32 devices in a mesh: pipe: 8 (over z, y), dp: 4 (over x, core).
Axes of the slice: x: 2, y: 2, z: 4, core: 2. Of those that a mesh axis runs over, the one named last changes fastest.
Arguments:
- act_in: bfloat16 [4, 8, 128, 8192], P('dp', 'pipe'), may hold values from -6 to 6
- stash_a: bfloat16 [4, 8, 128, 8192], P('dp', 'pipe'), may hold values from -6 to 6
- grad_in: bfloat16 [4, 8, 128, 8192], P('dp', 'pipe'), may hold values from -6 to 6
- text_emb: bfloat16 [4, 128, 8192], P('dp', None, 'pipe'), may hold values from -6 to 6
- enc_query: bfloat16 [4, 128, 3200], P('dp', 'pipe'), may hold values from -32 to 32
- enc_key: bfloat16 [4, 512, 3200], P('dp', 'pipe'), may hold values from -32 to 32
- enc_value: bfloat16 [4, 512, 3200], P('dp', 'pipe'), may hold values from -6 to 6
- tok_count: int32 [4, 8], P('dp', 'pipe'), may hold values from 1 to 16, as said below
- tok_offset: int32 [4, 8], P('dp', 'pipe'), may hold values from 0 to 112, as said below
- merge_gain: float32 [3200], replicated, may hold values from 0.1 to 1.9
- w_merge: bfloat16 [3200, 128], P(None, 'dp'), may hold values from -0.109375 to 0.109375
- w_vision: bfloat16 [128, 8192], P(None, 'pipe'), may hold values from -0.5 to 0.5
- norm_gain: float32 [8, 8192], P('pipe'), may hold values from 0.1 to 1.9
- w_down: bfloat16 [8, 8192, 128], P('pipe', 'dp'), may hold values from -0.0625 to 0.0625
- w_up: bfloat16 [8, 128, 8192], P('pipe', None, 'dp'), may hold values from -0.5 to 0.5
Outputs:
- fwd_out: bfloat16 [4, 8, 128, 8192], P('dp', 'pipe')
- bwd_out: bfloat16 [4, 8, 128, 8192], P('dp', 'pipe')
- grad_down: float32 [8, 8192, 128], P('pipe', 'dp')
- grad_up: float32 [8, 128, 8192], P('pipe', None, 'dp')
The draws below stay inside these ranges and needn't reach their ends.
Inputs may be any that keep to these rules, and one draw needn't show every extreme that they name: `tok_count`: in every replica some section has exactly 16 image tokens. Section p's tokens occupy positions tok_offset to tok_offset + tok_count - 1; these ranges lie within the sequence, are disjoint and rise with p.
All inputs are finite; a program needn't handle non-finite values.
Results may differ from the reference program's by a relative error of at most 0.017.
Values may be sent and summed in bfloat16 or wider, within the bound.
No kernel may reach another device: no remote copies, remote signals or barrier semaphores. Data moves between devices by JAX's collectives and lax.ppermute only.
A program may use at most 128 MiB of HBM per device.

```python
import jax
import jax.numpy as jnp
from jax import lax

D = 8192
R = 128
HEADS = 25
HEAD_DIM = 128
IMG = 64
S = 128
TMAX = 16
N_PIPE = 8
N_DP = 4


def section_layout(key):
    key_count, key_chosen, key_spacing = jax.random.split(key, 3)
    counts = jax.random.randint(key_count, (N_DP, N_PIPE), 1, TMAX + 1)
    chosen = jax.random.randint(key_chosen, (N_DP, 1), 0, N_PIPE)
    section_ids = jnp.arange(N_PIPE)[None, :]
    counts = jnp.where(section_ids == chosen, TMAX, counts)
    spacing = jax.random.randint(key_spacing, (N_DP, N_PIPE), 0, TMAX + 1) % (TMAX - counts + 1)
    spacing = jnp.where((section_ids == 0) | (section_ids == N_PIPE - 1), 0, spacing)
    offsets = section_ids * TMAX + spacing
    return (counts.astype(jnp.int32), offsets.astype(jnp.int32))


def draw_tok_count(key, part):
    layout = section_layout(key)
    return layout[0]


def draw_tok_offset(key, part):
    layout = section_layout(key)
    return layout[1]


def draw_enc_query(key, part):
    key = jax.random.fold_in(key, 1)
    width = HEADS * HEAD_DIM
    shape = (N_DP, N_PIPE * TMAX, width)
    return jnp.clip(jax.random.normal(key, shape, jnp.float32), -6.0, 6.0).astype(jnp.bfloat16)


def draw_enc_key(key, part):
    key = jax.random.fold_in(key, 2)
    shape = (N_DP, N_PIPE * IMG, HEADS * HEAD_DIM)
    noise = jax.random.normal(key, shape, jnp.float32)
    return jnp.clip(noise, -6.0, 6.0).astype(jnp.bfloat16)


def level_of(stream_key, dims, shards, low, largest):
    level = 1.0
    for position, shards_of in shards:
        steps = jax.random.uniform(jax.random.fold_in(jax.random.fold_in(stream_key, 6), position), (shards_of,), jnp.float32, low / len(shards), largest / len(shards))
        level = level * jnp.repeat(jnp.exp(steps), dims[position] // shards_of).reshape((-1,) + (1,) * (len(dims) - 1 - position))
    return level


def centred(rng, shape, deviation, bound, cuts=(), held_as=jnp.bfloat16):
    entries = jax.random.normal(rng, shape, jnp.float32) * deviation
    if len(cuts) > 0:
        entries = level_of(rng, shape, cuts, -0.22, 0.18) * entries
    return jnp.clip(entries, min=-bound, max=bound).astype(held_as)


def setup_inputs(seed: int = 0) -> dict:
    key_of = jax.random.split(jax.random.key(seed), 16)
    act_in = centred(key_of[0], (N_DP, N_PIPE, S, D), 1.0, 6.0, ((0, 4), (1, 8)))
    stash_a = centred(key_of[1], (N_DP, N_PIPE, S, D), 1.0, 6.0, ((0, 4), (1, 8)))
    grad_in = centred(key_of[2], (N_DP, N_PIPE, S, D), 1.0, 6.0, ((0, 4), (1, 8)))
    text_emb = centred(key_of[3], (N_DP, S, D), 1.0, 6.0, ((0, 4), (2, 8)))
    enc_query = draw_enc_query(jax.random.fold_in(key_of[15], 71), 0)
    enc_key = draw_enc_key(jax.random.fold_in(key_of[15], 71), 0)
    enc_value = centred(key_of[6], (N_DP, N_PIPE * IMG, HEADS * HEAD_DIM), 1.0, 6.0, ((0, 4), (1, 8)))
    tok_count = draw_tok_count(jax.random.fold_in(key_of[15], 71), 0)
    tok_offset = draw_tok_offset(jax.random.fold_in(key_of[15], 71), 0)
    merge_gain = jnp.clip(1.0 + 0.18 * jax.random.normal(key_of[9], (HEADS * HEAD_DIM,), jnp.float32), 0.1, 1.9)
    w_merge = centred(key_of[10], (HEADS * HEAD_DIM, R), (HEADS * HEAD_DIM) ** -0.5, 0.109375, ((1, 4),))
    w_vision = centred(key_of[11], (R, D), R ** -0.5, 0.5, ((1, 8),))
    norm_gain = jnp.clip(1.0 + 0.18 * jax.random.normal(key_of[12], (N_PIPE, D), jnp.float32), 0.1, 1.9)
    w_down = centred(key_of[13], (N_PIPE, D, R), D ** -0.5, 0.0625, ((0, 8), (1, 4)))
    w_up = centred(key_of[14], (N_PIPE, R, D), R ** -0.5, 0.5, ((0, 8), (2, 4)))
    return dict(act_in=act_in, stash_a=stash_a, grad_in=grad_in, text_emb=text_emb, enc_query=enc_query, enc_key=enc_key, enc_value=enc_value, tok_count=tok_count, tok_offset=tok_offset, merge_gain=merge_gain, w_merge=w_merge, w_vision=w_vision, norm_gain=norm_gain, w_down=w_down, w_up=w_up)


EPS = 1e-06

def swish(inner):
    return inner * jax.nn.sigmoid(inner)

def adapter_forward(x, gain, w_down, w_up):
    x32 = x.astype(jnp.float32)
    scale = lax.rsqrt(lax.optimization_barrier(jnp.mean(x32 * x32, -1, keepdims=True)) + EPS)
    normed = (x32 * scale * gain).astype(jnp.bfloat16)
    hidden = swish(jnp.dot(normed, w_down, preferred_element_type=jnp.float32)).astype(jnp.bfloat16)
    return (x32 + jnp.dot(hidden, w_up, preferred_element_type=jnp.float32)).astype(jnp.bfloat16)

def adapter_backward(x, grad_out, gain, w_down, w_up):
    x32 = x.astype(jnp.float32)
    scale = lax.rsqrt(lax.optimization_barrier(jnp.mean(x32 * x32, -1, keepdims=True)) + EPS)
    unit = x32 * scale
    normed = (unit * gain).astype(jnp.bfloat16)
    inner = jnp.dot(normed, w_down, preferred_element_type=jnp.float32)
    sig = jax.nn.sigmoid(inner)
    hidden = (inner * sig).astype(jnp.bfloat16)
    back_h = jnp.einsum('sd,rd->sr', grad_out.astype(jnp.float32), w_up.astype(jnp.float32))
    back_u = (back_h * sig * (1.0 + inner * (1.0 - sig))).astype(jnp.bfloat16)
    back_n = jnp.einsum('sr,dr->sd', back_u.astype(jnp.float32), w_down.astype(jnp.float32)) * gain
    back_x = scale * (back_n - unit * lax.optimization_barrier(jnp.mean(back_n * unit, -1, keepdims=True)))
    grad_x = (grad_out.astype(jnp.float32) + back_x).astype(jnp.bfloat16)
    down_term = jnp.einsum('sd,sr->dr', normed.astype(jnp.float32), back_u.astype(jnp.float32))
    up_term = jnp.einsum('sr,sd->rd', hidden.astype(jnp.float32), grad_out.astype(jnp.float32))
    return (grad_x, down_term, up_term)

def encode_section(query, keys, values):
    q3 = query.astype(jnp.float32).reshape(query.shape[0], HEADS, HEAD_DIM)
    k3 = keys.astype(jnp.float32).reshape(keys.shape[0], HEADS, HEAD_DIM)
    v3 = values.astype(jnp.float32).reshape(values.shape[0], HEADS, HEAD_DIM)
    scores = jnp.einsum('qhd,khd->hqk', q3, k3) * HEAD_DIM ** (-0.5)
    top = lax.optimization_barrier(jnp.max(scores, -1, keepdims=True))
    weights = jnp.exp(scores - top)
    probs = (weights / lax.optimization_barrier(jnp.sum(weights, -1, keepdims=True))).astype(jnp.bfloat16)
    attended = jnp.einsum('hqk,khd->qhd', probs.astype(jnp.float32), v3)
    return attended.reshape(query.shape[0], HEADS * HEAD_DIM).astype(jnp.bfloat16)

def merge_tokens(rows, gain, w_merge):
    x32 = rows.astype(jnp.float32)
    scale = lax.rsqrt(lax.optimization_barrier(jnp.mean(x32 * x32, -1, keepdims=True)) + EPS)
    normed = (x32 * scale * gain).astype(jnp.bfloat16)
    return jax.nn.gelu(jnp.dot(normed, w_merge, preferred_element_type=jnp.float32)).astype(jnp.bfloat16)

def place_rows(counts, offsets, seq_len, slots):
    slot_ids = jnp.arange(slots, dtype=jnp.int32)
    target = (offsets[:, None] + slot_ids[None, :]).reshape(-1)
    live = (slot_ids[None, :] < counts[:, None]).reshape(-1)
    return (jnp.arange(seq_len, dtype=jnp.int32)[:, None] == target[None, :]) & live[None, :]

def compose(vision, marked, text, w_vision):
    mapped = jnp.dot(vision, w_vision, preferred_element_type=jnp.float32)
    return jnp.where(marked[:, None], mapped, text.astype(jnp.float32)).astype(jnp.bfloat16)

def reference(act_in, stash_a, grad_in, text_emb, enc_query, enc_key, enc_value, tok_count, tok_offset, merge_gain, w_merge, w_vision, norm_gain, w_down, w_up):
    forward_all = jax.vmap(adapter_forward)
    backward_all = jax.vmap(adapter_backward)
    encode_all = jax.vmap(encode_section)
    total_down = jnp.zeros(w_down.shape, jnp.float32)
    total_up = jnp.zeros(w_up.shape, jnp.float32)
    fwd_list = []
    bwd_list = []
    for replica in range(N_DP):
        query = enc_query[replica].reshape(N_PIPE, TMAX, -1)
        keys = enc_key[replica].reshape(N_PIPE, IMG, -1)
        values = enc_value[replica].reshape(N_PIPE, IMG, -1)
        attended = encode_all(query, keys, values)
        tokens = merge_tokens(attended.reshape(N_PIPE * TMAX, -1), merge_gain, w_merge)
        placed = place_rows(tok_count[replica], tok_offset[replica], S, TMAX)
        vision = jnp.dot(placed.astype(jnp.bfloat16), tokens, preferred_element_type=jnp.float32).astype(jnp.bfloat16)
        marked = jnp.any(placed, 1)
        fresh = compose(vision, marked, text_emb[replica], w_vision)
        first = act_in[replica]
        out0 = forward_all(first, norm_gain, w_down, w_up)
        incoming = jnp.concatenate([fresh[None], out0[:-1]], 0)
        out1 = forward_all(incoming, norm_gain, w_down, w_up)
        final_out = adapter_forward(stash_a[replica, -1], norm_gain[-1], w_down[-1], w_up[-1])
        grad_first = jnp.concatenate([grad_in[replica, :-1], final_out[None]], 0)
        back0, down0, up0 = backward_all(stash_a[replica], grad_first, norm_gain, w_down, w_up)
        grad_second = jnp.concatenate([back0[1:], out0[-1:]], 0)
        back1, down1, up1 = backward_all(first, grad_second, norm_gain, w_down, w_up)
        total_down = total_down + down0 + down1
        total_up = total_up + up0 + up1
        fwd_list.append(out1)
        bwd_list.append(back1)
    return (jnp.stack(fwd_list, 0), jnp.stack(bwd_list, 0), total_down, total_up)
```

```python
import functools

import jax
import jax.numpy as jnp
from jax import lax
from jax.experimental import pallas as pl
from jax.experimental.pallas import tpu as pltpu
from jax.sharding import PartitionSpec as P

HEADS = 25
HEAD_DIM = 128
EPS = 1e-06
F32 = jnp.float32
BF16 = jnp.bfloat16
MIB = 1 << 20


def dot(a, b):
    return jnp.dot(a, b, preferred_element_type=F32)


def dot_nt(a, b):
    return lax.dot_general(a, b, (((1,), (1,)), ((), ())), preferred_element_type=F32)


def dot_tn(a, b):
    return lax.dot_general(a, b, (((0,), (0,)), ((), ())), preferred_element_type=F32)


def swap_cores(array):
    count = lax.axis_size("dp")
    return lax.ppermute(array, "dp", [(i, i ^ 1) for i in range(count)])


def shift_chips(array, by):
    count = lax.axis_size("dp")
    return lax.ppermute(array, "dp", [(i, (i + 2 * by) % count) for i in range(count)])


def tied(array, *others):
    return lax.optimization_barrier((array,) + others)[0]


def owners():
    me = lax.axis_index("dp")
    chips = lax.axis_size("dp") // 2
    chip, core = me // 2, me % 2
    out = []
    for k in range(chips):
        behind = lax.rem(chip - k + chips, chips)
        out += [behind * 2 + core, behind * 2 + 1 - core]
    return out


def targets():
    me = lax.axis_index("dp")
    chips = lax.axis_size("dp") // 2
    chip, core = me // 2, me % 2
    aheads = [lax.rem(chip + k, chips) for k in range(chips)]
    return [a * 2 + 1 - core for a in aheads], [a * 2 + core for a in aheads]


def far_pieces(shard):
    chips = lax.axis_size("dp") // 2
    return [shift_chips(shard, k) for k in range(1, chips)]


def with_far(shard, near, far):
    out = [shard, near]
    for piece in far:
        out += [piece, swap_cores(piece)]
    return out


def direct_pieces(shard):
    length = lax.axis_size("dp")
    out = [shard, swap_cores(shard)]
    for k in range(1, length // 2):
        pairs = [(i, ((i + 2 * k) % length) ^ 1) for i in range(length)]
        out += [shift_chips(shard, k), lax.ppermute(shard, "dp", pairs)]
    return out


def passed_along(array, by):
    length = lax.axis_size("pipe")
    pairs = [(i, i + by) for i in range(length) if 0 <= i + by < length]
    return lax.ppermute(array, "pipe", pairs)


def columns(index, size):
    return pl.ds(pl.multiple_of(index * size, size), size)


def chunk_of(width):
    return min(width, 512)


def call(kernel, scalars, ins, outs, scratch=(), in_specs=None, by_hand=(), outs_by_hand=(), cost=1, room=14):
    def whole(shape):
        return pl.BlockSpec(shape, lambda i, s, n=len(shape): (0,) * n)

    anywhere = pl.BlockSpec(memory_space=pl.ANY)
    specs = [anywhere if at in by_hand else whole(a.shape) for at, a in enumerate(ins)]
    for at, spec in (in_specs or {}).items():
        specs[at] = spec
    return pl.pallas_call(
        kernel,
        grid_spec=pltpu.PrefetchScalarGridSpec(
            num_scalar_prefetch=1,
            grid=(1,),
            in_specs=specs,
            out_specs=[anywhere if at in outs_by_hand else whole(o.shape) for at, o in enumerate(outs)],
            scratch_shapes=list(scratch),
        ),
        out_shape=list(outs),
        compiler_params=pltpu.CompilerParams(vmem_limit_bytes=room * MIB),
        cost_estimate=pl.CostEstimate(flops=cost, bytes_accessed=1, transcendentals=0),
    )(scalars, *ins)


def shape(dims, dtype):
    return jax.ShapeDtypeStruct(dims, dtype)


def started(source, target, sem):
    copy = pltpu.make_async_copy(source, target, sem)
    copy.start()
    return copy


def hidden_of(inner):
    return (inner * jax.nn.sigmoid(inner)).astype(BF16)


def factor_of(inner, back_h):
    sig = jax.nn.sigmoid(inner)
    return (back_h * sig * (1.0 + inner * (1.0 - sig))).astype(BF16)


def scale_into(x_ref, width):
    size = chunk_of(width)

    def add(j, acc):
        x = x_ref[:, columns(j, size)].astype(F32)
        return acc + x * x

    total = lax.fori_loop(0, width // size, add, jnp.zeros((x_ref.shape[0], size), F32))
    return lax.rsqrt(jnp.sum(total, -1, keepdims=True) / width + EPS)


def prep_kernel(s_ref, x_ref, gain_ref, normed_ref, scale_ref):
    rows, width = x_ref.shape
    size = chunk_of(width)
    scale = scale_into(x_ref, width)
    scale_ref[...] = jnp.broadcast_to(scale, (rows, 128))

    def write(j, carry):
        cols = columns(j, size)
        x = x_ref[:, cols].astype(F32)
        normed_ref[:, cols] = (x * scale * gain_ref[:, cols]).astype(BF16)
        return carry

    lax.fori_loop(0, width // size, write, 0)


def inner_from(s_ref, normed_ref, downs):
    width = downs[0].shape[0]
    inner = dot(normed_ref[:, columns(s_ref[2], width)], downs[0][...])
    for k in range(1, len(downs)):
        inner += dot(normed_ref[:, columns(s_ref[2 + k], width)], downs[k][...])
    return inner


def inner_kernel(count, s_ref, normed_ref, *refs):
    refs[count][...] = inner_from(s_ref, normed_ref, refs[:count])


def forward_kernel(count, s_ref, normed_ref, first_own_ref, up_own_ref, *refs):
    downs, (inner_ref, out_ref) = refs[:count], refs[count:]
    width = downs[0].shape[0]
    inner = inner_from(s_ref, normed_ref, downs)
    inner_ref[...] = inner
    hidden = hidden_of(inner)
    size = chunk_of(width)
    for j in range(width // size):
        cols = pl.ds(j * size, size)
        x = first_own_ref[:, cols].astype(F32)
        out_ref[:, cols] = (x + dot(hidden, up_own_ref[:, cols])).astype(BF16)


def forward_into(s_ref, x_ref, hidden, up, out_ref, rows):
    count, _, width = up.shape
    size = chunk_of(width)
    for k in range(count):
        for j in range(width // size):
            cols = pl.ds(pl.multiple_of(s_ref[2 + k] * width + j * size, size), size)
            x = x_ref[:, cols].astype(F32)
            out_ref[rows, cols] = (x + dot(hidden, up[k, :, pl.ds(j * size, size)])).astype(BF16)


def factor_from(s_ref, grad_ref, rows, inner, up):
    count, _, width = up.shape
    back_h = dot_nt(grad_ref[rows, columns(s_ref[2], width)], up[0])
    for k in range(1, count):
        back_h += dot_nt(grad_ref[rows, columns(s_ref[2 + k], width)], up[k])
    return factor_of(inner, back_h)


def back_kernel(count, given, s_ref, x_hbm, came_hbm, inner_ref, scale_ref, gain_ref, *refs):
    refs = list(refs)
    factor_in = refs.pop(0) if given else None
    ups, downs, refs = refs[:count], refs[count:2 * count], refs[2 * count:]
    out_hbm = refs.pop(0)
    factor_out = None if given else refs.pop(0)
    x_ref, grad_ref, out_ref, up, down, sems = refs
    rows, full = x_ref.shape
    width = up.shape[2]
    size = chunk_of(width)
    every = pl.ds(0, rows)
    is_last = s_ref[0] == 1
    grad_copy = started(came_hbm, grad_ref, sems.at[0])

    def load_ups():
        return [started(ups[k], up.at[k], sems.at[2 + k]) for k in range(count)]

    up_copies = [] if given else load_ups()
    x_copy = started(x_hbm, x_ref, sems.at[1])
    down_copies = [started(downs[k], down.at[k], sems.at[2 + count + k]) for k in range(count)]
    inner = inner_ref[...]
    grad_copy.wait()
    for copy in up_copies:
        copy.wait()
    if given:
        x_copy.wait()

    @pl.when(is_last)
    def _():
        if given:
            for copy in load_ups():
                copy.wait()
        else:
            x_copy.wait()
        forward_into(s_ref, x_ref, hidden_of(inner), up, grad_ref, every)

    if given:
        factor = factor_in[...]
    else:
        factor = factor_from(s_ref, grad_ref, every, inner, up)
        factor_out[...] = factor

        @pl.when(jnp.logical_not(is_last))
        def _():
            x_copy.wait()

    mean = jnp.sum(factor.astype(F32) * inner, -1, keepdims=True) / full
    scale = scale_ref[:, 0:1]
    bend = scale * scale * mean
    out_copies = []
    for k in range(count):
        down_copies[k].wait()
        for j in range(width // size):
            cols = pl.ds(pl.multiple_of(s_ref[2 + k] * width + j * size, size), size)
            back_n = dot_nt(factor, down[k, pl.ds(j * size, size), :]) * gain_ref[:, cols]
            x = x_ref[:, cols].astype(F32)
            grad = grad_ref[:, cols].astype(F32)
            out_ref[:, cols] = (grad + (scale * back_n - bend * x)).astype(BF16)
        cols = columns(s_ref[2 + k], width)
        out_copies.append(
            started(out_ref.at[:, cols], out_hbm.at[:, cols], sems.at[2 + 2 * count + k])
        )
    for copy in out_copies:
        copy.wait()


def rest_kernel(count, s_ref, first_ref, inner_ref, *refs):
    ups, out_refs = refs[:count], refs[count:]
    width = ups[0].shape[1]
    size = chunk_of(width)
    hidden = hidden_of(inner_ref[...])
    places = [(ref, at) for ref in out_refs for at in range(ref.shape[1] // width)]
    for k, (out_ref, at) in enumerate(places):
        for j in range(width // size):
            cols = pl.ds(pl.multiple_of(s_ref[3 + k] * width + j * size, size), size)
            x = first_ref[:, cols].astype(F32)
            out_ref[:, pl.ds(at * width + j * size, size)] = (
                x + dot(hidden, ups[k][:, pl.ds(j * size, size)])
            ).astype(BF16)


def up_kernel(
    count, s_ref, stash_hbm, first_hbm, came0_hbm, came1_hbm, inner_s_ref, inner_a_ref, *refs
):
    ups, refs = refs[:count], refs[count:]
    factor_ref, slices, (grads, x_ref, up, sems) = refs[0], refs[1:1 + count], refs[1 + count:]
    rows, _ = x_ref.shape
    width = up.shape[2]
    size = chunk_of(width)
    first_rows, second_rows = pl.ds(0, rows), pl.ds(rows, rows)
    copies = [started(came1_hbm, grads.at[second_rows], sems.at[0])]
    copies += [started(ups[k], up.at[k], sems.at[2 + k]) for k in range(count)]
    copies += [started(came0_hbm, grads.at[first_rows], sems.at[1])]
    hidden_s, hidden_a = hidden_of(inner_s_ref[...]), hidden_of(inner_a_ref[...])
    for copy in copies:
        copy.wait()

    @pl.when(s_ref[0] == 1)
    def _():
        started(stash_hbm, x_ref, sems.at[0]).wait()
        forward_into(s_ref, x_ref, hidden_s, up, grads, first_rows)
        started(first_hbm, x_ref, sems.at[0]).wait()
        forward_into(s_ref, x_ref, hidden_a, up, grads, second_rows)

    factor_ref[...] = factor_from(s_ref, grads, second_rows, inner_a_ref[...], up)
    both = jnp.concatenate([hidden_s, hidden_a], 0).astype(F32).T.astype(BF16)
    for k, ref in enumerate(slices):
        base = s_ref[2 + count + k] * width
        for j in range(width // size):
            cols = pl.ds(pl.multiple_of(base + j * size, size), size)
            ref[:, pl.ds(j * size, size)] = dot(both, grads[:, cols]).astype(ref.dtype)


def down_kernel(count, s_ref, normed_s_ref, normed_a_ref, factor0_ref, factor1_ref, *refs):
    width = refs[0].shape[0]
    size = chunk_of(width)
    factor0, factor1 = factor0_ref[...], factor1_ref[...]
    for k, ref in enumerate(refs):
        base = s_ref[2 + count + k] * width
        for j in range(width // size):
            cols = pl.ds(pl.multiple_of(base + j * size, size), size)
            term = dot_tn(normed_s_ref[:, cols], factor0) + dot_tn(normed_a_ref[:, cols], factor1)
            ref[pl.ds(j * size, size), :] = term.astype(ref.dtype)


def compose_into(x_ref, order, blocks, texts, maps, part_ref, sems):
    rows, _ = x_ref.shape
    size = part_ref.shape[3]
    copies = []
    for half, refs in enumerate((texts, maps)):
        slabs = [(ref, k) for ref in refs for k in range(ref.shape[0])]
        for at, (ref, k) in enumerate(slabs):
            copies.append(started(ref.at[k], part_ref.at[half, at], sems.at[half, at]))
    flat = [ref[k].astype(F32) for ref in blocks for k in range(ref.shape[0])]
    slots = flat[0].shape[0] // 2
    row = lax.broadcasted_iota(jnp.int32, (rows, slots), 0).astype(F32)
    slot = lax.broadcasted_iota(jnp.int32, (rows, slots), 1).astype(F32)
    vision = jnp.zeros((rows, flat[0].shape[1]), F32)
    marked = jnp.zeros((rows, 1), F32)
    for block in flat:
        number, first_row = block[slots:slots + 1, 0:1], block[slots:slots + 1, 1:2]
        placed = jnp.where((row == first_row + slot) & (slot < number), 1.0, 0.0)
        vision += dot(placed.astype(BF16), block[:slots].astype(BF16))
        marked += jnp.sum(placed, -1, keepdims=True)
    vision = vision.astype(BF16)
    for at, section in enumerate(order):
        copies[at].wait()
        copies[len(order) + at].wait()
        mapped = dot(vision, part_ref[1, at])
        text = part_ref[0, at].astype(F32)
        x_ref[:, pl.ds(section * size, size)] = jnp.where(marked > 0.5, mapped, text).astype(BF16)


def last_kernel(count, order, n_arrays, s_ref, gain_ref, own_hbm, *refs):
    refs = list(refs)
    rests, refs = refs[:2], refs[2:]
    blocks, texts, maps = (refs[at * n_arrays:(at + 1) * n_arrays] for at in range(3))
    refs = refs[3 * n_arrays:]
    downs, ups = refs[:count], refs[count:2 * count]
    out_hbm, x_ref, out_ref, up, down, part_ref, sems, part_sems = refs[2 * count:]
    width = up.shape[2]
    rows, full = x_ref.shape
    size = chunk_of(width)

    @pl.when(s_ref[1] == 1)
    def _():
        compose_into(x_ref, order, blocks, texts, maps, part_ref, part_sems)

    @pl.when(s_ref[1] == 0)
    def _():
        copies = [started(own_hbm, x_ref.at[:, columns(s_ref[2], width)], sems.at[0])]
        for ref in rests:
            for at in range(ref.shape[1] // width):
                k = len(copies)
                copies.append(
                    started(
                        ref.at[:, pl.ds(at * width, width)],
                        x_ref.at[:, columns(s_ref[2 + k], width)],
                        sems.at[k],
                    )
                )
        for copy in copies:
            copy.wait()

    down_copies = [started(downs[k], down.at[k], sems.at[count + k]) for k in range(count)]
    up_copies = [started(ups[k], up.at[k], sems.at[2 * count + k]) for k in range(count)]
    scale = scale_into(x_ref, full)
    inner = jnp.zeros((rows, down.shape[2]), F32)
    for k in range(count):
        down_copies[k].wait()
        for j in range(width // size):
            cols = pl.ds(pl.multiple_of(s_ref[2 + k] * width + j * size, size), size)
            normed = (x_ref[:, cols].astype(F32) * scale * gain_ref[:, cols]).astype(BF16)
            inner += dot(normed, down[k, pl.ds(j * size, size), :])
    hidden = hidden_of(inner)
    out_copies = []
    for k in range(count):
        up_copies[k].wait()
        for j in range(width // size):
            cols = pl.ds(pl.multiple_of(s_ref[2 + k] * width + j * size, size), size)
            x = x_ref[:, cols].astype(F32)
            out_ref[:, cols] = (x + dot(hidden, up[k, :, pl.ds(j * size, size)])).astype(BF16)
        cols = columns(s_ref[2 + k], width)
        out_copies.append(
            started(out_ref.at[:, cols], out_hbm.at[:, cols], sems.at[3 * count + k])
        )
    for copy in out_copies:
        copy.wait()


def encode_section(query, keys, values):
    q3 = query.reshape(query.shape[0], HEADS, HEAD_DIM)
    k3 = keys.reshape(keys.shape[0], HEADS, HEAD_DIM)
    v3 = values.reshape(values.shape[0], HEADS, HEAD_DIM)
    scores = jnp.einsum("qhd,khd->hqk", q3, k3, preferred_element_type=F32) * HEAD_DIM ** (-0.5)
    top = jnp.max(scores, -1, keepdims=True)
    weights = jnp.exp(scores - top)
    probs = (weights / jnp.sum(weights, -1, keepdims=True)).astype(BF16)
    attended = jnp.einsum("hqk,khd->qhd", probs, v3, preferred_element_type=F32)
    return attended.reshape(query.shape[0], HEADS * HEAD_DIM).astype(BF16)


def tree_round(held, step):
    length = lax.axis_size("pipe")
    pairs = [(i + at + step, i + at) for i in range(0, length, 2 * step) for at in (0, 1)]
    packed = jnp.stack(held)
    return packed, lax.ppermute(packed, "pipe", pairs)


def tree_start(arrays, step=2):
    length = lax.axis_size("pipe")
    arrays = list(arrays)
    while step < length:
        packed, came = tree_round([a[k] for a in arrays for k in range(a.shape[0])], step)
        if 2 * step == length:
            early = to_first(packed)
        arrays.append(came)
        step *= 2
    order = [0]
    for at in range(1, length.bit_length() - 1):
        order = order + [section + 2**at for section in order]
    return arrays, early, came, order + [section + 1 for section in order]


def to_first(array):
    return lax.ppermute(array, "pipe", [(1, 0)])


def tokens_of(attended, merge_gain, merge_pieces, tok_count, tok_offset):
    slots = attended.shape[0]
    x32 = attended.astype(F32)
    scale = lax.rsqrt(jnp.mean(x32 * x32, -1, keepdims=True) + EPS)
    normed = (x32 * scale * merge_gain).astype(BF16)
    merged = [jax.nn.gelu(dot_nt(normed, piece)).astype(BF16) for piece in merge_pieces]
    size = merged[0].shape[1]
    tokens = jnp.zeros((slots, size * len(merged)), BF16)
    for piece, owner in zip(merged, owners()):
        tokens = lax.dynamic_update_slice_in_dim(tokens, piece, owner * size, 1)
    place = jnp.concatenate([tok_count, tok_offset], 1).astype(BF16)
    place = jnp.pad(place, ((0, slots - 1), (0, tokens.shape[1] - 2)))
    return jnp.concatenate([tokens, place], 0)


def body(
    act_in,
    stash_a,
    grad_in,
    text_emb,
    enc_query,
    enc_key,
    enc_value,
    tok_count,
    tok_offset,
    merge_gain,
    w_merge,
    w_vision,
    norm_gain,
    w_down,
    w_up,
):
    section = lax.axis_index("pipe")
    is_last = section == lax.axis_size("pipe") - 1
    count = lax.axis_size("dp")
    chips = count // 2
    gain = norm_gain
    first, stash, grad = act_in[0, 0], stash_a[0, 0], grad_in[0, 0]
    down, up = w_down[0], w_up[0]
    rows, full = first.shape
    rank, width = up.shape
    sent_to, kept_by = targets()
    scalars = jnp.stack(
        [is_last.astype(jnp.int32), (section == 0).astype(jnp.int32)]
        + owners() + sent_to + kept_by
    ).astype(jnp.int32)

    def vmem(dims):
        return pltpu.VMEM(dims, BF16)

    act, ups_shape, downs_shape = (rows, full), (count, rank, width), (count, width, rank)

    down_far = far_pieces(down)
    text_arrays, text_early, text_waiting, order = tree_start([text_emb])
    _, map_came = tree_round([w_vision], 2)
    down_near, up_near = swap_cores(down), swap_cores(up)
    prep_outs = [shape(act, BF16), shape((rows, 128), F32)]
    normed_a, scale_a = call(prep_kernel, scalars, [first, gain], prep_outs)
    normed_s, scale_s = call(prep_kernel, scalars, [stash, gain], prep_outs)
    up = tied(up, normed_a, normed_s, *down_far)
    up_far = far_pieces(up)
    downs = with_far(down, down_near, down_far)

    inner_a, out_own = call(
        functools.partial(forward_kernel, count), scalars, [normed_a, first, up] + downs,
        [shape((rows, rank), F32), shape((rows, width), BF16)],
        in_specs={1: pl.BlockSpec((rows, width), lambda i, s: (0, s[2]))},
    )
    came_own = passed_along(out_own, 1)
    text_arrays += [text_early, to_first(tied(text_waiting, out_own))]
    (inner_s,) = call(
        functools.partial(inner_kernel, count), scalars, [tied(normed_s, out_own)] + downs,
        [shape((rows, rank), F32)],
    )
    query = tied(enc_query[0], out_own)
    attended = encode_section(query, enc_key[0], enc_value[0])

    ups = with_far(up, up_near, up_far)
    back_scratch = [vmem(act)] * 3 + [
        vmem(ups_shape), vmem(downs_shape), pltpu.SemaphoreType.DMA((2 + 3 * count,))
    ]
    hands = set(range(5, 5 + 2 * count)) | {0, 1}
    back0, factor0 = call(
        functools.partial(back_kernel, count, False), scalars,
        [tied(stash, came_own, attended, map_came, *text_arrays[1:]), grad, inner_s, scale_s, gain] + ups + downs,
        [shape(act, BF16), shape((rows, rank), BF16)],
        scratch=back_scratch, by_hand=hands, outs_by_hand={0},
    )
    after = passed_along(back0, -1)

    groups = [1, count - 2]
    rests = call(
        functools.partial(rest_kernel, count - 1), scalars,
        [tied(first, factor0), inner_a] + ups[1:], [shape((rows, group * width), BF16) for group in groups],
    )
    merge_own = tied(w_merge, factor0).T
    merge_pieces = direct_pieces(merge_own)

    tokens = tokens_of(attended, merge_gain, merge_pieces, tok_count, tok_offset)

    after = tied(after, tokens, *rests)
    came_rests, before = [], after
    for rest in rests:
        before = passed_along(tied(rest, before), 1)
        came_rests.append(before)
    map_arrays, map_early, map_waiting, _ = tree_start([w_vision[None], tied(map_came, after)], 4)
    map_arrays += [map_early, to_first(map_waiting)]

    factor1, *up_slices = call(
        functools.partial(up_kernel, count), scalars,
        [stash, first, grad, after, inner_s, inner_a] + ups,
        [shape((rows, rank), BF16)] + [shape((rank, width), BF16)] * chips
        + [shape((rank, width), F32)] * chips,
        scratch=[
            vmem((2 * rows, full)), vmem(act), vmem(ups_shape),
            pltpu.SemaphoreType.DMA((2 + count,)),
        ],
        by_hand={0, 1, 2, 3} | set(range(6, 6 + count)), room=18,
    )
    down_slices = call(
        functools.partial(down_kernel, count), scalars, [normed_s, normed_a, factor0, factor1],
        [shape((width, rank), BF16)] * chips + [shape((width, rank), F32)] * chips,
        room=20,
    )
    sums = []
    for slices in (up_slices, down_slices):
        sent, kept = slices[:chips], slices[chips:]
        terms = [kept[0] + swap_cores(sent[0]).astype(F32)]
        for k in range(chips - 1, 0, -1):
            far = (kept[k] + swap_cores(sent[k]).astype(F32)).astype(BF16)
            terms.append(shift_chips(far, k))
        sums.append(terms)
    token_arrays, token_early, token_waiting, _ = tree_start([tied(tokens, after)[None]])
    (back1,) = call(
        functools.partial(back_kernel, count, True), scalars,
        [first, after, inner_a, scale_a, gain, tied(factor1, down_slices[0])] + ups + downs,
        [shape(act, BF16)],
        scratch=back_scratch, by_hand=set(range(6, 6 + 2 * count)) | {0, 1}, outs_by_hand={0},
    )

    token_arrays += [token_early, to_first(token_waiting)]
    n_arrays, n_pipe = len(token_arrays), lax.axis_size("pipe")
    blocks_at = 2 + len(came_rests)
    (out1,) = call(
        functools.partial(last_kernel, count, order, n_arrays), scalars,
        [gain, came_own] + came_rests + token_arrays + text_arrays + map_arrays + downs + ups, [shape(act, BF16)],
        scratch=[vmem(act)] * 2 + [
            vmem(ups_shape), vmem(downs_shape), vmem((2, n_pipe) + w_vision.shape),
            pltpu.SemaphoreType.DMA((4 * count,)), pltpu.SemaphoreType.DMA((2, n_pipe)),
        ],
        by_hand=set(range(1, blocks_at)) | set(range(blocks_at + n_arrays, blocks_at + 3 * n_arrays + 2 * count)), outs_by_hand={0},
        room=18,
    )
    grad_up, grad_down = (
        sum((tied(term, out1).astype(F32) for term in terms[1:]), terms[0]) for terms in sums
    )
    return (out1[None, None], back1[None, None], grad_down[None], grad_up[None])


def solution(mesh):
    in_specs = (
        P("dp", "pipe", None, None),
        P("dp", "pipe", None, None),
        P("dp", "pipe", None, None),
        P("dp", None, "pipe"),
        P("dp", "pipe", None),
        P("dp", "pipe", None),
        P("dp", "pipe", None),
        P("dp", "pipe"),
        P("dp", "pipe"),
        P(),
        P(None, "dp"),
        P(None, "pipe"),
        P("pipe", None),
        P("pipe", "dp", None),
        P("pipe", None, "dp"),
    )
    out_specs = (
        P("dp", "pipe", None, None),
        P("dp", "pipe", None, None),
        P("pipe", "dp", None),
        P("pipe", None, "dp"),
    )
    return jax.shard_map(body, mesh=mesh, in_specs=in_specs, out_specs=out_specs, check_vma=False)
```

```python
import functools

import jax
import jax.numpy as jnp
from jax import lax
from jax.experimental import pallas as pl
from jax.experimental.pallas import tpu as pltpu
from jax.sharding import PartitionSpec as P

HEADS = 25
HEAD_DIM = 128
EPS = 1e-06
F32 = jnp.float32
BF16 = jnp.bfloat16
MIB = 1 << 20


def dot(a, b):
    return jnp.dot(a, b, preferred_element_type=F32)


def dot_nt(a, b):
    return lax.dot_general(a, b, (((1,), (1,)), ((), ())), preferred_element_type=F32)


def dot_tn(a, b):
    return lax.dot_general(a, b, (((0,), (0,)), ((), ())), preferred_element_type=F32)


def swap_cores(array):
    count = lax.axis_size("dp")
    return lax.ppermute(array, "dp", [(i, i ^ 1) for i in range(count)])


def shift_chips(array, by):
    count = lax.axis_size("dp")
    return lax.ppermute(array, "dp", [(i, (i + 2 * by) % count) for i in range(count)])


def tied(array, *others):
    return lax.optimization_barrier((array,) + others)[0]


def owners():
    me = lax.axis_index("dp")
    chips = lax.axis_size("dp") // 2
    chip, core = me // 2, me % 2
    out = []
    for k in range(chips):
        behind = lax.rem(chip - k + chips, chips)
        out += [behind * 2 + core, behind * 2 + 1 - core]
    return out


def targets():
    me = lax.axis_index("dp")
    chips = lax.axis_size("dp") // 2
    chip, core = me // 2, me % 2
    aheads = [lax.rem(chip + k, chips) for k in range(chips)]
    return [a * 2 + 1 - core for a in aheads], [a * 2 + core for a in aheads]


def far_pieces(shard):
    chips = lax.axis_size("dp") // 2
    return [shift_chips(shard, k) for k in range(1, chips)]


def with_far(shard, near, far):
    out = [shard, near]
    for piece in far:
        out += [piece, swap_cores(piece)]
    return out


def direct_pieces(shard):
    length = lax.axis_size("dp")
    out = [shard, swap_cores(shard)]
    for k in range(1, length // 2):
        pairs = [(i, ((i + 2 * k) % length) ^ 1) for i in range(length)]
        out += [shift_chips(shard, k), lax.ppermute(shard, "dp", pairs)]
    return out


def passed_along(array, by):
    length = lax.axis_size("pipe")
    pairs = [(i, i + by) for i in range(length) if 0 <= i + by < length]
    return lax.ppermute(array, "pipe", pairs)


def columns(index, size):
    return pl.ds(pl.multiple_of(index * size, size), size)


def chunk_of(width):
    return min(width, 512)


def call(kernel, scalars, ins, outs, scratch=(), in_specs=None, by_hand=(), in_hbm=(), outs_by_hand=(), room=14, flops=1):
    def whole(shape):
        return pl.BlockSpec(shape, lambda i, s, n=len(shape): (0,) * n)

    anywhere, hbm = pl.BlockSpec(memory_space=pl.ANY), pl.BlockSpec(memory_space=pltpu.HBM)
    specs = [anywhere if at in by_hand else whole(a.shape) for at, a in enumerate(ins)]
    specs = [hbm if at in in_hbm else spec for at, spec in enumerate(specs)]
    for at, spec in (in_specs or {}).items():
        specs[at] = spec
    return pl.pallas_call(
        kernel,
        grid_spec=pltpu.PrefetchScalarGridSpec(
            num_scalar_prefetch=1,
            grid=(1,),
            in_specs=specs,
            out_specs=[anywhere if at in outs_by_hand else whole(o.shape) for at, o in enumerate(outs)],
            scratch_shapes=list(scratch),
        ),
        out_shape=list(outs),
        compiler_params=pltpu.CompilerParams(vmem_limit_bytes=room * MIB),
        cost_estimate=pl.CostEstimate(flops=flops, bytes_accessed=1, transcendentals=0),
    )(scalars, *ins)


def shape(dims, dtype):
    return jax.ShapeDtypeStruct(dims, dtype)


def started(source, target, sem):
    copy = pltpu.make_async_copy(source, target, sem)
    copy.start()
    return copy


def hidden_of(inner):
    return (inner * jax.nn.sigmoid(inner)).astype(BF16)


def factor_of(inner, back_h):
    sig = jax.nn.sigmoid(inner)
    return (back_h * sig * (1.0 + inner * (1.0 - sig))).astype(BF16)


def scale_into(x_ref, width):
    size = chunk_of(width)

    def add(j, acc):
        x = x_ref[:, columns(j, size)].astype(F32)
        return acc + x * x

    total = lax.fori_loop(0, width // size, add, jnp.zeros((x_ref.shape[0], size), F32))
    return lax.rsqrt(jnp.sum(total, -1, keepdims=True) / width + EPS)


def prep_kernel(s_ref, x_ref, gain_ref, normed_ref, scale_ref):
    rows, width = x_ref.shape
    size = chunk_of(width)
    scale = scale_into(x_ref, width)
    scale_ref[...] = jnp.broadcast_to(scale, (rows, 128))

    def write(j, carry):
        cols = columns(j, size)
        x = x_ref[:, cols].astype(F32)
        normed_ref[:, cols] = (x * scale * gain_ref[:, cols]).astype(BF16)
        return carry

    lax.fori_loop(0, width // size, write, 0)


def inner_from(s_ref, normed_ref, downs):
    width = downs[0].shape[0]
    inner = dot(normed_ref[:, columns(s_ref[2], width)], downs[0][...])
    for k in range(1, len(downs)):
        inner += dot(normed_ref[:, columns(s_ref[2 + k], width)], downs[k][...])
    return inner


def inner_kernel(count, s_ref, normed_ref, *refs):
    refs[count][...] = inner_from(s_ref, normed_ref, refs[:count])


def forward_kernel(count, s_ref, normed_ref, first_own_ref, up_own_ref, *refs):
    downs, (inner_ref, *out_refs) = refs[:count], refs[count:]
    width = out_refs[0].shape[1]
    inner = inner_from(s_ref, normed_ref, downs)
    inner_ref[...] = inner
    hidden = hidden_of(inner)
    size = chunk_of(width)
    for k, out_ref in enumerate(out_refs):
        for j in range(width // size):
            cols = pl.ds(k * width + j * size, size)
            x = first_own_ref[:, cols].astype(F32)
            out_ref[:, pl.ds(j * size, size)] = (x + dot(hidden, up_own_ref[:, cols])).astype(BF16)


def forward_into(s_ref, x_ref, hidden, up, out_ref, rows):
    count, _, width = up.shape
    size = chunk_of(width)
    for k in range(count):
        for j in range(width // size):
            cols = pl.ds(pl.multiple_of(s_ref[2 + k] * width + j * size, size), size)
            x = x_ref[:, cols].astype(F32)
            out_ref[rows, cols] = (x + dot(hidden, up[k, :, pl.ds(j * size, size)])).astype(BF16)


def factor_from(s_ref, grad_ref, rows, inner, up):
    count, _, width = up.shape
    back_h = dot_nt(grad_ref[rows, columns(s_ref[2], width)], up[0])
    for k in range(1, count):
        back_h += dot_nt(grad_ref[rows, columns(s_ref[2 + k], width)], up[k])
    return factor_of(inner, back_h)


def back_kernel(count, given, s_ref, x_hbm, came_hbm, inner_ref, scale_ref, gain_ref, *refs):
    refs = list(refs)
    factor_in = refs.pop(0) if given else None
    ups, downs, refs = refs[:count], refs[count:2 * count], refs[2 * count:]
    out_hbm = refs.pop(0)
    factor_out = None if given else refs.pop(0)
    x_ref, grad_ref, out_ref, up, down, sems = refs
    rows, full = x_ref.shape
    width = up.shape[2]
    size = chunk_of(width)
    every = pl.ds(0, rows)
    is_last = s_ref[0] == 1
    grad_copy = started(came_hbm, grad_ref, sems.at[0])

    def load_ups():
        return [started(ups[k], up.at[k], sems.at[2 + k]) for k in range(count)]

    up_copies = [] if given else load_ups()
    x_copy = started(x_hbm, x_ref, sems.at[1])
    down_copies = [started(downs[k], down.at[k], sems.at[2 + count + k]) for k in range(count)]
    inner = inner_ref[...]
    grad_copy.wait()
    for copy in up_copies:
        copy.wait()
    if given:
        x_copy.wait()

    @pl.when(is_last)
    def _():
        if given:
            for copy in load_ups():
                copy.wait()
        else:
            x_copy.wait()
        forward_into(s_ref, x_ref, hidden_of(inner), up, grad_ref, every)

    if given:
        factor = factor_in[...]
    else:
        factor = factor_from(s_ref, grad_ref, every, inner, up)
        factor_out[...] = factor

        @pl.when(jnp.logical_not(is_last))
        def _():
            x_copy.wait()

    mean = jnp.sum(factor.astype(F32) * inner, -1, keepdims=True) / full
    scale = scale_ref[:, 0:1]
    bend = scale * scale * mean
    out_copies = []
    for k in range(count):
        down_copies[k].wait()
        for j in range(width // size):
            cols = pl.ds(pl.multiple_of(s_ref[2 + k] * width + j * size, size), size)
            back_n = dot_nt(factor, down[k, pl.ds(j * size, size), :]) * gain_ref[:, cols]
            x = x_ref[:, cols].astype(F32)
            grad = grad_ref[:, cols].astype(F32)
            out_ref[:, cols] = (grad + (scale * back_n - bend * x)).astype(BF16)
        cols = columns(s_ref[2 + k], width)
        out_copies.append(
            started(out_ref.at[:, cols], out_hbm.at[:, cols], sems.at[2 + 2 * count + k])
        )
    for copy in out_copies:
        copy.wait()


def rest_kernel(count, s_ref, first_ref, inner_ref, *refs):
    ups, out_refs = refs[:count], refs[count:]
    width = ups[0].shape[1]
    size = chunk_of(width)
    hidden = hidden_of(inner_ref[...])
    places = [(ref, at) for ref in out_refs for at in range(ref.shape[1] // width)]
    for k, (out_ref, at) in enumerate(places):
        for j in range(width // size):
            cols = pl.ds(pl.multiple_of(s_ref[3 + k] * width + j * size, size), size)
            x = first_ref[:, cols].astype(F32)
            out_ref[:, pl.ds(at * width + j * size, size)] = (
                x + dot(hidden, ups[k][:, pl.ds(j * size, size)])
            ).astype(BF16)


def terms_kernel(
    count, s_ref, stash_hbm, first_hbm, came0_hbm, came1_hbm, inner_s_ref, inner_a_ref,
    factor0_ref, scale_s_ref, scale_a_ref, gain_ref, *refs
):
    ups, refs = refs[:count], refs[count:]
    factor_ref, slices, (grads, x_s, x_a, up, sems) = refs[0], refs[1:1 + count], refs[1 + count:]
    rows, _ = x_s.shape
    width = up.shape[2]
    size = chunk_of(width)
    first_rows, second_rows = pl.ds(0, rows), pl.ds(rows, rows)
    copies = [started(came1_hbm, grads.at[second_rows], sems.at[0])]
    copies += [started(ups[k], up.at[k], sems.at[4 + k]) for k in range(count)]
    copies += [started(came0_hbm, grads.at[first_rows], sems.at[1])]
    late = [started(stash_hbm, x_s, sems.at[2]), started(first_hbm, x_a, sems.at[3])]
    hidden_s, hidden_a = hidden_of(inner_s_ref[...]), hidden_of(inner_a_ref[...])
    for copy in copies:
        copy.wait()

    @pl.when(s_ref[0] == 1)
    def _():
        for copy in late:
            copy.wait()
        forward_into(s_ref, x_s, hidden_s, up, grads, first_rows)
        forward_into(s_ref, x_a, hidden_a, up, grads, second_rows)

    factor1 = factor_from(s_ref, grads, second_rows, inner_a_ref[...], up)
    factor_ref[...] = factor1
    hidden = jnp.concatenate([hidden_s, hidden_a], 0).astype(F32).T.astype(BF16)
    factor = jnp.concatenate([factor0_ref[...], factor1], 0).astype(F32).T.astype(BF16)
    chunks = [(k, j) for k in range(count) for j in range(width // size)]

    def place(k, j):
        base = s_ref[2 + count + k] * width
        return pl.ds(pl.multiple_of(base + j * size, size), size), pl.ds(j * size, size)

    for k, j in chunks:
        cols, at = place(k, j)
        slices[k][0, :, at] = dot(hidden, grads[:, cols]).astype(slices[k].dtype)

    @pl.when(s_ref[0] == 0)
    def _():
        for copy in late:
            copy.wait()

    pairs = ((x_s, scale_s_ref[:, 0:1]), (x_a, scale_a_ref[:, 0:1]))
    for k, j in chunks:
        cols, at = place(k, j)
        normed = [(x[:, cols].astype(F32) * scale * gain_ref[:, cols]).astype(BF16) for x, scale in pairs]
        slices[k][1, :, at] = dot(factor, jnp.concatenate(normed, 0)).astype(slices[k].dtype)


def compose_into(rank, slots, x_ref, order, slabs, part_ref, sems):
    rows, _ = x_ref.shape
    size = part_ref.shape[2]
    text_at = part_ref.shape[1] - rows
    near, parts = slabs[:6], slabs[6:]
    places = [(0, rank, size), (rank, text_at - rank, rank), (text_at, rows, size)]
    copies = []
    for refs, (start, length, lanes) in zip((near[2:4], near[4:6], near[0:2]), places):
        for at in range(4):
            target = part_ref.at[at, pl.ds(start, length), pl.ds(0, lanes)]
            copies.append(started(refs[at // 2].at[at % 2], target, sems.at[len(copies)]))
    for at in range(4, len(order)):
        source = parts[at // 2 - 2].at[at % 2]
        copies.append(started(source, part_ref.at[at], sems.at[len(copies)]))
    for copy in copies:
        copy.wait()
    row = lax.broadcasted_iota(jnp.int32, (rows, slots), 0).astype(F32)
    slot = lax.broadcasted_iota(jnp.int32, (rows, slots), 1).astype(F32)
    vision = jnp.zeros((rows, rank), F32)
    marked = jnp.zeros((rows, 1), F32)
    for at in range(len(order)):
        block = part_ref[at, rank:text_at, :rank].astype(F32)
        number, first_row = block[slots:slots + 1, 0:1], block[slots:slots + 1, 1:2]
        placed = jnp.where((row == first_row + slot) & (slot < number), 1.0, 0.0)
        vision += dot(placed.astype(BF16), block[:slots].astype(BF16))
        marked += jnp.sum(placed, -1, keepdims=True)
    vision = vision.astype(BF16)
    for at, section in enumerate(order):
        mapped = dot(vision, part_ref[at, :rank, :])
        text = part_ref[at, text_at:, :].astype(F32)
        x_ref[:, pl.ds(section * size, size)] = jnp.where(marked > 0.5, mapped, text).astype(BF16)


def last_kernel(count, order, n_arrays, slots, s_ref, gain_ref, *refs):
    refs = list(refs)
    owns, rests, refs = refs[:2], refs[2:3], refs[3:]
    slabs, refs = refs[:n_arrays], refs[n_arrays:]
    downs, ups = refs[:count], refs[count:2 * count]
    out_hbm, x_ref, out_ref, up, down, part_ref, sems, part_sems = refs[2 * count:]
    width = up.shape[2]
    rows, full = x_ref.shape
    size = chunk_of(width)

    @pl.when(s_ref[1] == 1)
    def _():
        compose_into(down.shape[2], slots, x_ref, order, slabs, part_ref, part_sems)

    @pl.when(s_ref[1] == 0)
    def _():
        half = width // 2
        copies = [
            started(owns[k], x_ref.at[:, columns(2 * s_ref[2] + k, half)], sems.at[k])
            for k in range(2)
        ]
        for k in range(1, count):
            source = rests[0].at[:, pl.ds((k - 1) * width, width)]
            copies.append(
                started(source, x_ref.at[:, columns(s_ref[2 + k], width)], sems.at[1 + k])
            )
        for copy in copies:
            copy.wait()

    down_copies = [started(downs[k], down.at[k], sems.at[count + 1 + k]) for k in range(count)]
    up_copies = [started(ups[k], up.at[k], sems.at[2 * count + 1 + k]) for k in range(count)]
    scale = scale_into(x_ref, full)
    inner = jnp.zeros((rows, down.shape[2]), F32)
    for k in range(count):
        down_copies[k].wait()
        for j in range(width // size):
            cols = pl.ds(pl.multiple_of(s_ref[2 + k] * width + j * size, size), size)
            normed = (x_ref[:, cols].astype(F32) * scale * gain_ref[:, cols]).astype(BF16)
            inner += dot(normed, down[k, pl.ds(j * size, size), :])
    hidden = hidden_of(inner)
    out_copies = []
    for k in range(count):
        up_copies[k].wait()
        for j in range(width // size):
            cols = pl.ds(pl.multiple_of(s_ref[2 + k] * width + j * size, size), size)
            x = x_ref[:, cols].astype(F32)
            out_ref[:, cols] = (x + dot(hidden, up[k, :, pl.ds(j * size, size)])).astype(BF16)
        cols = columns(s_ref[2 + k], width)
        out_copies.append(
            started(out_ref.at[:, cols], out_hbm.at[:, cols], sems.at[3 * count + 1 + k])
        )
    for copy in out_copies:
        copy.wait()


def encode_section(query, keys, values):
    q3 = query.reshape(query.shape[0], HEADS, HEAD_DIM)
    k3 = keys.reshape(keys.shape[0], HEADS, HEAD_DIM)
    v3 = values.reshape(values.shape[0], HEADS, HEAD_DIM)
    scores = jnp.einsum("qhd,khd->hqk", q3, k3, preferred_element_type=F32) * HEAD_DIM ** (-0.5)
    top = jnp.max(scores, -1, keepdims=True)
    weights = jnp.exp(scores - top)
    probs = (weights / jnp.sum(weights, -1, keepdims=True)).astype(BF16)
    attended = jnp.einsum("hqk,khd->qhd", probs, v3, preferred_element_type=F32)
    return attended.reshape(query.shape[0], HEADS * HEAD_DIM).astype(BF16)


def pairs_of(array):
    length = lax.axis_size("pipe")
    pairs = [(i + at + 2, i + at) for i in range(0, length, 4) for at in (0, 1)]
    return lax.ppermute(array, "pipe", pairs)


def to_first(packed, sections, hold=None):
    out = []
    for section in sections:
        sent = packed
        if hold is not None and section % 4 == 1:
            sent = tied(packed, *hold)
        out.append(lax.ppermute(sent, "pipe", [(section, 0)]))
        if hold is not None and section % 4 == 1:
            hold = [out[-1]]
    return out


def tokens_of(attended, merge_gain, merge_pieces, tok_count, tok_offset):
    slots = attended.shape[0]
    x32 = attended.astype(F32)
    scale = lax.rsqrt(jnp.mean(x32 * x32, -1, keepdims=True) + EPS)
    normed = (x32 * scale * merge_gain).astype(BF16)
    merged = [jax.nn.gelu(dot_nt(normed, piece)).astype(BF16) for piece in merge_pieces]
    size = merged[0].shape[1]
    tokens = jnp.zeros((slots, size * len(merged)), BF16)
    for piece, owner in zip(merged, owners()):
        tokens = lax.dynamic_update_slice_in_dim(tokens, piece, owner * size, 1)
    place = jnp.concatenate([tok_count, tok_offset], 1).astype(BF16)
    place = jnp.pad(place, ((0, slots - 1), (0, tokens.shape[1] - 2)))
    block = jnp.concatenate([tokens, place], 0)
    return jnp.pad(block, ((0, -block.shape[0] % 16), (0, 0)))


def body(
    act_in,
    stash_a,
    grad_in,
    text_emb,
    enc_query,
    enc_key,
    enc_value,
    tok_count,
    tok_offset,
    merge_gain,
    w_merge,
    w_vision,
    norm_gain,
    w_down,
    w_up,
):
    section = lax.axis_index("pipe")
    is_last = section == lax.axis_size("pipe") - 1
    count = lax.axis_size("dp")
    chips = count // 2
    gain = norm_gain
    first, stash, grad = act_in[0, 0], stash_a[0, 0], grad_in[0, 0]
    down, up = w_down[0], w_up[0]
    rows, full = first.shape
    rank, width = up.shape
    n_pipe = lax.axis_size("pipe")
    sent_to, kept_by = targets()
    scalars = jnp.stack(
        [is_last.astype(jnp.int32), (section == 0).astype(jnp.int32)]
        + owners() + sent_to + kept_by
    ).astype(jnp.int32)

    def vmem(dims):
        return pltpu.VMEM(dims, BF16)

    act, ups_shape, downs_shape = (rows, full), (count, rank, width), (count, width, rank)

    down_far = far_pieces(down)
    far_sections = [i + at for i in range(4, n_pipe, 4) for at in (1, 0)]
    order = [at + more for at in [0, 1] + far_sections for more in (0, 2)]
    text_came, map_came = pairs_of(text_emb[0]), pairs_of(w_vision)
    down_near, up_near = swap_cores(down), swap_cores(up)
    prep_outs = [shape(act, BF16), shape((rows, 128), F32)]
    normed_a, scale_a = call(prep_kernel, scalars, [first, gain], prep_outs)
    down_far = [tied(piece, normed_a, text_came, map_came) for piece in down_far]
    up = tied(up, *down_far)
    up_far = far_pieces(up)
    downs = with_far(down, down_near, down_far)

    inner_a, out_own, out_own_end = call(
        functools.partial(forward_kernel, count), scalars, [normed_a, first, up] + downs,
        [shape((rows, rank), F32)] + [shape((rows, width // 2), BF16)] * 2,
        in_specs={1: pl.BlockSpec((rows, width), lambda i, s: (0, s[2]))},
    )
    came_owns = [passed_along(out_own, 1)]
    came_owns.append(passed_along(tied(out_own_end, came_owns[0]), 1))
    normed_s, scale_s = call(prep_kernel, tied(scalars, out_own), [stash, gain], prep_outs)
    text_near = jnp.stack([text_emb[0], tied(text_came, out_own)])
    (text_early,) = to_first(text_near, [1])
    map_near = jnp.stack([w_vision, map_came])
    (map_early,) = to_first(tied(map_near, text_early), [1])
    (inner_s,) = call(
        functools.partial(inner_kernel, count), scalars, [normed_s] + downs,
        [shape((rows, rank), F32)],
    )
    ups = with_far(up, up_near, up_far)
    back_scratch = [vmem(act)] * 3 + [
        vmem(ups_shape), vmem(downs_shape), pltpu.SemaphoreType.DMA((2 + 3 * count,))
    ]
    hands = set(range(5, 5 + 2 * count))
    back0, factor0 = call(
        functools.partial(back_kernel, count, False), tied(scalars, *came_owns),
        [stash, grad, inner_s, scale_s, gain] + ups + downs,
        [shape(act, BF16), shape((rows, rank), BF16)],
        scratch=back_scratch, by_hand=hands, in_hbm={0, 1}, outs_by_hand={0},
    )
    after = passed_along(back0, -1)

    groups = [count - 1]
    rests = call(
        functools.partial(rest_kernel, count - 1), tied(scalars, factor0),
        [first, inner_a] + ups[1:], [shape((rows, group * width), BF16) for group in groups],
    )
    encoder = lax.optimization_barrier((enc_query[0], enc_key[0], enc_value[0], factor0))[:3]
    attended = encode_section(*encoder)
    merge_own = tied(w_merge, factor0, map_early).T
    merge_pieces = direct_pieces(merge_own)

    tokens = tokens_of(attended, merge_gain, merge_pieces, tok_count, tok_offset)

    tokens_came = pairs_of(tokens)
    pad = ((0, 0), (0, w_vision.shape[1] - tokens.shape[1]))
    after = tied(after, tokens, *rests)
    came_rests, before = [], after
    for rest in rests:
        before = passed_along(tied(rest, before), 1)
        came_rests.append(before)
    sent = jnp.stack(
        [
            jnp.concatenate([rows_of, jnp.pad(tokens_of_it, pad), text_of], 0)
            for rows_of, tokens_of_it, text_of in (
                (w_vision, tokens, text_emb[0]), (map_came, tokens_came, text_came)
            )
        ]
    )
    parts = to_first(tied(sent, after), far_sections)
    tokens_near = tied(jnp.stack([tokens, tokens_came]), after)
    near = [text_near, text_early, map_near, map_early, tokens_near] + to_first(tokens_near, [1])

    both = (2, rank, width)
    factor1, *slices = call(
        functools.partial(terms_kernel, count), scalars,
        [stash, first, grad, after, inner_s, inner_a, factor0, scale_s, scale_a, gain] + ups,
        [shape((rows, rank), BF16)] + [shape(both, BF16)] * chips + [shape(both, F32)] * chips,
        scratch=[
            vmem((2 * rows, full)), vmem(act), vmem(act), vmem(ups_shape),
            pltpu.SemaphoreType.DMA((4 + count,)),
        ],
        by_hand={0, 1, 2, 3} | set(range(10, 10 + count)), room=58,
    )
    other, kept = slices[:chips], slices[chips:]
    total = kept[0] + swap_cores(other[0]).astype(F32)
    terms = []
    for k in range(chips - 1, 0, -1):
        far = (kept[k] + swap_cores(other[k]).astype(F32)).astype(BF16)
        terms.append(shift_chips(far, k))
    (back1,) = call(
        functools.partial(back_kernel, count, True), scalars,
        [first, after, inner_a, scale_a, gain, tied(factor1, total)] + ups + downs,
        [shape(act, BF16)],
        scratch=back_scratch, by_hand={1}, in_hbm=set(range(6, 6 + 2 * count)) | {0},
        outs_by_hand={0},
    )

    n_arrays = len(near) + len(parts)
    blocks_at = 1 + len(came_owns) + len(came_rests)
    (out1,) = call(
        functools.partial(last_kernel, count, order, n_arrays, enc_query.shape[1]), tied(scalars, back1),
        [gain] + came_owns + came_rests + near + parts + downs + ups, [shape(act, BF16)],
        scratch=[vmem(act)] * 2 + [
            vmem(ups_shape), vmem(downs_shape), vmem((n_pipe,) + sent.shape[1:]),
            pltpu.SemaphoreType.DMA((4 * count + 1,)), pltpu.SemaphoreType.DMA((n_pipe + 8,)),
        ],
        by_hand=set(range(1, blocks_at + n_arrays)),
        in_hbm=set(range(blocks_at + n_arrays, blocks_at + n_arrays + 2 * count)),
        outs_by_hand={0},
        room=18, flops=5 * 10**9,
    )
    for term in terms:
        total = total + tied(term, out1).astype(F32)
    grad_up, grad_down = total[0], total[1].T
    return (out1[None, None], back1[None, None], grad_down[None], grad_up[None])


def solution(mesh):
    in_specs = (
        P("dp", "pipe", None, None),
        P("dp", "pipe", None, None),
        P("dp", "pipe", None, None),
        P("dp", None, "pipe"),
        P("dp", "pipe", None),
        P("dp", "pipe", None),
        P("dp", "pipe", None),
        P("dp", "pipe"),
        P("dp", "pipe"),
        P(),
        P(None, "dp"),
        P(None, "pipe"),
        P("pipe", None),
        P("pipe", "dp", None),
        P("pipe", None, "dp"),
    )
    out_specs = (
        P("dp", "pipe", None, None),
        P("dp", "pipe", None, None),
        P("pipe", "dp", None),
        P("pipe", None, "dp"),
    )
    return jax.shard_map(body, mesh=mesh, in_specs=in_specs, out_specs=out_specs, check_vma=False)
```

```python
import functools

import jax
import jax.numpy as jnp
from jax import lax
from jax.experimental import pallas as pl
from jax.experimental.pallas import tpu as pltpu
from jax.sharding import PartitionSpec as P

HEADS = 25
HEAD_DIM = 128
EPS = 1e-06
F32 = jnp.float32
BF16 = jnp.bfloat16
MIB = 1 << 20


def dot(a, b):
    return jnp.dot(a, b, preferred_element_type=F32)


def dot_nt(a, b):
    return lax.dot_general(a, b, (((1,), (1,)), ((), ())), preferred_element_type=F32)


def dot_tn(a, b):
    return lax.dot_general(a, b, (((0,), (0,)), ((), ())), preferred_element_type=F32)


def swap_cores(array):
    count = lax.axis_size("dp")
    return lax.ppermute(array, "dp", [(i, i ^ 1) for i in range(count)])


def shift_chips(array, by):
    count = lax.axis_size("dp")
    return lax.ppermute(array, "dp", [(i, (i + 2 * by) % count) for i in range(count)])


def tied(array, *others):
    return lax.optimization_barrier((array,) + others)[0]


def owners():
    me = lax.axis_index("dp")
    chips = lax.axis_size("dp") // 2
    chip, core = me // 2, me % 2
    out = []
    for k in range(chips):
        behind = lax.rem(chip - k + chips, chips)
        out += [behind * 2 + core, behind * 2 + 1 - core]
    return out


def targets():
    me = lax.axis_index("dp")
    chips = lax.axis_size("dp") // 2
    chip, core = me // 2, me % 2
    aheads = [lax.rem(chip + k, chips) for k in range(chips)]
    return [a * 2 + 1 - core for a in aheads], [a * 2 + core for a in aheads]


def far_pieces(shard):
    chips = lax.axis_size("dp") // 2
    return [shift_chips(shard, k) for k in range(1, chips)]


def with_far(shard, near, far):
    out = [shard, near]
    for piece in far:
        out += [piece, swap_cores(piece)]
    return out


def direct_pieces(shard):
    length = lax.axis_size("dp")
    out = [shard, swap_cores(shard)]
    for k in range(1, length // 2):
        pairs = [(i, ((i + 2 * k) % length) ^ 1) for i in range(length)]
        out += [shift_chips(shard, k), lax.ppermute(shard, "dp", pairs)]
    return out


def passed_along(array, by):
    length = lax.axis_size("pipe")
    pairs = [(i, i + by) for i in range(length) if 0 <= i + by < length]
    return lax.ppermute(array, "pipe", pairs)


def columns(index, size):
    return pl.ds(pl.multiple_of(index * size, size), size)


def chunk_of(width):
    return min(width, 512)


def call(kernel, scalars, ins, outs, scratch=(), in_specs=None, by_hand=(), outs_by_hand=(), cost=1, room=14):
    def whole(shape):
        return pl.BlockSpec(shape, lambda i, s, n=len(shape): (0,) * n)

    anywhere = pl.BlockSpec(memory_space=pl.ANY)
    specs = [anywhere if at in by_hand else whole(a.shape) for at, a in enumerate(ins)]
    for at, spec in (in_specs or {}).items():
        specs[at] = spec
    return pl.pallas_call(
        kernel,
        grid_spec=pltpu.PrefetchScalarGridSpec(
            num_scalar_prefetch=1,
            grid=(1,),
            in_specs=specs,
            out_specs=[anywhere if at in outs_by_hand else whole(o.shape) for at, o in enumerate(outs)],
            scratch_shapes=list(scratch),
        ),
        out_shape=list(outs),
        compiler_params=pltpu.CompilerParams(vmem_limit_bytes=room * MIB),
        cost_estimate=pl.CostEstimate(flops=cost, bytes_accessed=1, transcendentals=0),
    )(scalars, *ins)


def shape(dims, dtype):
    return jax.ShapeDtypeStruct(dims, dtype)


def started(source, target, sem):
    copy = pltpu.make_async_copy(source, target, sem)
    copy.start()
    return copy


def hidden_of(inner):
    return (inner * jax.nn.sigmoid(inner)).astype(BF16)


def factor_of(inner, back_h):
    sig = jax.nn.sigmoid(inner)
    return (back_h * sig * (1.0 + inner * (1.0 - sig))).astype(BF16)


def scale_into(x_ref, width):
    size = chunk_of(width)

    def add(j, acc):
        x = x_ref[:, columns(j, size)].astype(F32)
        return acc + x * x

    total = lax.fori_loop(0, width // size, add, jnp.zeros((x_ref.shape[0], size), F32))
    return lax.rsqrt(jnp.sum(total, -1, keepdims=True) / width + EPS)


def prep_kernel(s_ref, x_ref, gain_ref, normed_ref, scale_ref):
    rows, width = x_ref.shape
    size = chunk_of(width)
    scale = scale_into(x_ref, width)
    scale_ref[...] = jnp.broadcast_to(scale, (rows, 128))

    def write(j, carry):
        cols = columns(j, size)
        x = x_ref[:, cols].astype(F32)
        normed_ref[:, cols] = (x * scale * gain_ref[:, cols]).astype(BF16)
        return carry

    lax.fori_loop(0, width // size, write, 0)


def inner_from(s_ref, normed_ref, downs):
    width = downs[0].shape[0]
    inner = dot(normed_ref[:, columns(s_ref[2], width)], downs[0][...])
    for k in range(1, len(downs)):
        inner += dot(normed_ref[:, columns(s_ref[2 + k], width)], downs[k][...])
    return inner


def inner_kernel(count, s_ref, normed_ref, *refs):
    refs[count][...] = inner_from(s_ref, normed_ref, refs[:count])


def forward_kernel(count, s_ref, normed_ref, first_own_ref, up_own_ref, *refs):
    downs, (inner_ref, out_ref) = refs[:count], refs[count:]
    width = downs[0].shape[0]
    inner = inner_from(s_ref, normed_ref, downs)
    inner_ref[...] = inner
    hidden = hidden_of(inner)
    size = chunk_of(width)
    for j in range(width // size):
        cols = pl.ds(j * size, size)
        x = first_own_ref[:, cols].astype(F32)
        out_ref[:, cols] = (x + dot(hidden, up_own_ref[:, cols])).astype(BF16)


def forward_into(s_ref, x_ref, hidden, up, out_ref, rows):
    count, _, width = up.shape
    size = chunk_of(width)
    for k in range(count):
        for j in range(width // size):
            cols = pl.ds(pl.multiple_of(s_ref[2 + k] * width + j * size, size), size)
            x = x_ref[:, cols].astype(F32)
            out_ref[rows, cols] = (x + dot(hidden, up[k, :, pl.ds(j * size, size)])).astype(BF16)


def factor_from(s_ref, grad_ref, rows, inner, up):
    count, _, width = up.shape
    back_h = dot_nt(grad_ref[rows, columns(s_ref[2], width)], up[0])
    for k in range(1, count):
        back_h += dot_nt(grad_ref[rows, columns(s_ref[2 + k], width)], up[k])
    return factor_of(inner, back_h)


def back_kernel(count, given, s_ref, x_hbm, came_hbm, inner_ref, scale_ref, gain_ref, *refs):
    refs = list(refs)
    factor_in = refs.pop(0) if given else None
    ups, downs, refs = refs[:count], refs[count:2 * count], refs[2 * count:]
    out_hbm = refs.pop(0)
    factor_out = None if given else refs.pop(0)
    x_ref, grad_ref, out_ref, up, down, sems = refs
    rows, full = x_ref.shape
    width = up.shape[2]
    size = chunk_of(width)
    every = pl.ds(0, rows)
    is_last = s_ref[0] == 1
    grad_copy = started(came_hbm, grad_ref, sems.at[0])

    def load_ups():
        return [started(ups[k], up.at[k], sems.at[2 + k]) for k in range(count)]

    up_copies = [] if given else load_ups()
    x_copy = started(x_hbm, x_ref, sems.at[1])
    down_copies = [started(downs[k], down.at[k], sems.at[2 + count + k]) for k in range(count)]
    inner = inner_ref[...]
    grad_copy.wait()
    for copy in up_copies:
        copy.wait()
    if given:
        x_copy.wait()

    @pl.when(is_last)
    def _():
        if given:
            for copy in load_ups():
                copy.wait()
        else:
            x_copy.wait()
        forward_into(s_ref, x_ref, hidden_of(inner), up, grad_ref, every)

    if given:
        factor = factor_in[...]
    else:
        factor = factor_from(s_ref, grad_ref, every, inner, up)
        factor_out[...] = factor

        @pl.when(jnp.logical_not(is_last))
        def _():
            x_copy.wait()

    mean = jnp.sum(factor.astype(F32) * inner, -1, keepdims=True) / full
    scale = scale_ref[:, 0:1]
    bend = scale * scale * mean
    out_copies = []
    for k in range(count):
        down_copies[k].wait()
        for j in range(width // size):
            cols = pl.ds(pl.multiple_of(s_ref[2 + k] * width + j * size, size), size)
            back_n = dot_nt(factor, down[k, pl.ds(j * size, size), :]) * gain_ref[:, cols]
            x = x_ref[:, cols].astype(F32)
            grad = grad_ref[:, cols].astype(F32)
            out_ref[:, cols] = (grad + (scale * back_n - bend * x)).astype(BF16)
        cols = columns(s_ref[2 + k], width)
        out_copies.append(
            started(out_ref.at[:, cols], out_hbm.at[:, cols], sems.at[2 + 2 * count + k])
        )
    for copy in out_copies:
        copy.wait()


def rest_kernel(count, s_ref, first_ref, inner_ref, *refs):
    ups, out_refs = refs[:count], refs[count:]
    width = ups[0].shape[1]
    size = chunk_of(width)
    hidden = hidden_of(inner_ref[...])
    places = [(ref, at) for ref in out_refs for at in range(ref.shape[1] // width)]
    for k, (out_ref, at) in enumerate(places):
        for j in range(width // size):
            cols = pl.ds(pl.multiple_of(s_ref[3 + k] * width + j * size, size), size)
            x = first_ref[:, cols].astype(F32)
            out_ref[:, pl.ds(at * width + j * size, size)] = (
                x + dot(hidden, ups[k][:, pl.ds(j * size, size)])
            ).astype(BF16)


def terms_kernel(
    count, s_ref, stash_hbm, first_hbm, came0_hbm, came1_hbm, inner_s_ref, inner_a_ref,
    factor0_ref, scale_s_ref, scale_a_ref, gain_ref, *refs
):
    ups, refs = refs[:count], refs[count:]
    factor_ref, up_slices, down_slices = refs[0], refs[1:1 + count], refs[1 + count:1 + 2 * count]
    grads, x_s, x_a, up, sems = refs[1 + 2 * count:]
    rows, _ = x_s.shape
    width = up.shape[2]
    size = chunk_of(width)
    first_rows, second_rows = pl.ds(0, rows), pl.ds(rows, rows)
    copies = [started(came1_hbm, grads.at[second_rows], sems.at[0])]
    copies += [started(ups[k], up.at[k], sems.at[4 + k]) for k in range(count)]
    copies += [started(came0_hbm, grads.at[first_rows], sems.at[1])]
    late = [started(stash_hbm, x_s, sems.at[2]), started(first_hbm, x_a, sems.at[3])]
    hidden_s, hidden_a = hidden_of(inner_s_ref[...]), hidden_of(inner_a_ref[...])
    for copy in copies:
        copy.wait()

    @pl.when(s_ref[0] == 1)
    def _():
        for copy in late:
            copy.wait()
        forward_into(s_ref, x_s, hidden_s, up, grads, first_rows)
        forward_into(s_ref, x_a, hidden_a, up, grads, second_rows)

    factor1 = factor_from(s_ref, grads, second_rows, inner_a_ref[...], up)
    factor_ref[...] = factor1
    hidden = jnp.concatenate([hidden_s, hidden_a], 0).astype(F32).T.astype(BF16)
    for k, ref in enumerate(up_slices):
        base = s_ref[2 + count + k] * width
        for j in range(width // size):
            cols = pl.ds(pl.multiple_of(base + j * size, size), size)
            ref[:, pl.ds(j * size, size)] = dot(hidden, grads[:, cols]).astype(ref.dtype)
    factor = jnp.concatenate([factor0_ref[...], factor1], 0)

    @pl.when(s_ref[0] == 0)
    def _():
        for copy in late:
            copy.wait()

    pairs = ((x_s, scale_s_ref[:, 0:1]), (x_a, scale_a_ref[:, 0:1]))
    for k, ref in enumerate(down_slices):
        base = s_ref[2 + count + k] * width
        for j in range(width // size):
            cols = pl.ds(pl.multiple_of(base + j * size, size), size)
            normed = jnp.concatenate(
                [(x[:, cols].astype(F32) * scale * gain_ref[:, cols]).astype(BF16) for x, scale in pairs], 0
            )
            ref[pl.ds(j * size, size), :] = dot_tn(normed, factor).astype(ref.dtype)


def compose_into(x_ref, order, blocks, texts, maps, part_ref, sems):
    rows, _ = x_ref.shape
    size = part_ref.shape[3]
    copies = []
    for half, refs in enumerate((texts, maps)):
        slabs = [(ref, k) for ref in refs for k in range(ref.shape[0])]
        for at, (ref, k) in enumerate(slabs):
            copies.append(started(ref.at[k], part_ref.at[half, at], sems.at[half, at]))
    flat = [ref[k].astype(F32) for ref in blocks for k in range(ref.shape[0])]
    slots = flat[0].shape[0] // 2
    row = lax.broadcasted_iota(jnp.int32, (rows, slots), 0).astype(F32)
    slot = lax.broadcasted_iota(jnp.int32, (rows, slots), 1).astype(F32)
    vision = jnp.zeros((rows, flat[0].shape[1]), F32)
    marked = jnp.zeros((rows, 1), F32)
    for block in flat:
        number, first_row = block[slots:slots + 1, 0:1], block[slots:slots + 1, 1:2]
        placed = jnp.where((row == first_row + slot) & (slot < number), 1.0, 0.0)
        vision += dot(placed.astype(BF16), block[:slots].astype(BF16))
        marked += jnp.sum(placed, -1, keepdims=True)
    vision = vision.astype(BF16)
    for at, section in enumerate(order):
        copies[at].wait()
        copies[len(order) + at].wait()
        mapped = dot(vision, part_ref[1, at])
        text = part_ref[0, at].astype(F32)
        x_ref[:, pl.ds(section * size, size)] = jnp.where(marked > 0.5, mapped, text).astype(BF16)


def last_kernel(count, order, n_arrays, s_ref, gain_ref, own_hbm, *refs):
    refs = list(refs)
    rests, refs = refs[:2], refs[2:]
    blocks, texts, maps = (refs[at * n_arrays:(at + 1) * n_arrays] for at in range(3))
    refs = refs[3 * n_arrays:]
    downs, ups = refs[:count], refs[count:2 * count]
    out_hbm, x_ref, out_ref, up, down, part_ref, sems, part_sems = refs[2 * count:]
    width = up.shape[2]
    rows, full = x_ref.shape
    size = chunk_of(width)

    @pl.when(s_ref[1] == 1)
    def _():
        compose_into(x_ref, order, blocks, texts, maps, part_ref, part_sems)

    @pl.when(s_ref[1] == 0)
    def _():
        copies = [started(own_hbm, x_ref.at[:, columns(s_ref[2], width)], sems.at[0])]
        for ref in rests:
            for at in range(ref.shape[1] // width):
                k = len(copies)
                copies.append(
                    started(
                        ref.at[:, pl.ds(at * width, width)],
                        x_ref.at[:, columns(s_ref[2 + k], width)],
                        sems.at[k],
                    )
                )
        for copy in copies:
            copy.wait()

    down_copies = [started(downs[k], down.at[k], sems.at[count + k]) for k in range(count)]
    up_copies = [started(ups[k], up.at[k], sems.at[2 * count + k]) for k in range(count)]
    scale = scale_into(x_ref, full)
    inner = jnp.zeros((rows, down.shape[2]), F32)
    for k in range(count):
        down_copies[k].wait()
        for j in range(width // size):
            cols = pl.ds(pl.multiple_of(s_ref[2 + k] * width + j * size, size), size)
            normed = (x_ref[:, cols].astype(F32) * scale * gain_ref[:, cols]).astype(BF16)
            inner += dot(normed, down[k, pl.ds(j * size, size), :])
    hidden = hidden_of(inner)
    out_copies = []
    for k in range(count):
        up_copies[k].wait()
        for j in range(width // size):
            cols = pl.ds(pl.multiple_of(s_ref[2 + k] * width + j * size, size), size)
            x = x_ref[:, cols].astype(F32)
            out_ref[:, cols] = (x + dot(hidden, up[k, :, pl.ds(j * size, size)])).astype(BF16)
        cols = columns(s_ref[2 + k], width)
        out_copies.append(
            started(out_ref.at[:, cols], out_hbm.at[:, cols], sems.at[3 * count + k])
        )
    for copy in out_copies:
        copy.wait()


def encode_section(query, keys, values):
    q3 = query.reshape(query.shape[0], HEADS, HEAD_DIM)
    k3 = keys.reshape(keys.shape[0], HEADS, HEAD_DIM)
    v3 = values.reshape(values.shape[0], HEADS, HEAD_DIM)
    scores = jnp.einsum("qhd,khd->hqk", q3, k3, preferred_element_type=F32) * HEAD_DIM ** (-0.5)
    top = jnp.max(scores, -1, keepdims=True)
    weights = jnp.exp(scores - top)
    probs = (weights / jnp.sum(weights, -1, keepdims=True)).astype(BF16)
    attended = jnp.einsum("hqk,khd->qhd", probs, v3, preferred_element_type=F32)
    return attended.reshape(query.shape[0], HEADS * HEAD_DIM).astype(BF16)


def tree_round(held, step):
    length = lax.axis_size("pipe")
    pairs = [(i + at + step, i + at) for i in range(0, length, 2 * step) for at in (0, 1)]
    packed = jnp.stack(held)
    return packed, lax.ppermute(packed, "pipe", pairs)


def tree_start(arrays, step=2):
    length = lax.axis_size("pipe")
    arrays = list(arrays)
    while step < length:
        packed, came = tree_round([a[k] for a in arrays for k in range(a.shape[0])], step)
        if 2 * step == length:
            early = to_first(packed)
        arrays.append(came)
        step *= 2
    order = [0]
    for at in range(1, length.bit_length() - 1):
        order = order + [section + 2**at for section in order]
    return arrays, early, came, order + [section + 1 for section in order]


def to_first(array):
    return lax.ppermute(array, "pipe", [(1, 0)])


def tokens_of(attended, merge_gain, merge_pieces, tok_count, tok_offset):
    slots = attended.shape[0]
    x32 = attended.astype(F32)
    scale = lax.rsqrt(jnp.mean(x32 * x32, -1, keepdims=True) + EPS)
    normed = (x32 * scale * merge_gain).astype(BF16)
    merged = [jax.nn.gelu(dot_nt(normed, piece)).astype(BF16) for piece in merge_pieces]
    size = merged[0].shape[1]
    tokens = jnp.zeros((slots, size * len(merged)), BF16)
    for piece, owner in zip(merged, owners()):
        tokens = lax.dynamic_update_slice_in_dim(tokens, piece, owner * size, 1)
    place = jnp.concatenate([tok_count, tok_offset], 1).astype(BF16)
    place = jnp.pad(place, ((0, slots - 1), (0, tokens.shape[1] - 2)))
    return jnp.concatenate([tokens, place], 0)


def body(
    act_in,
    stash_a,
    grad_in,
    text_emb,
    enc_query,
    enc_key,
    enc_value,
    tok_count,
    tok_offset,
    merge_gain,
    w_merge,
    w_vision,
    norm_gain,
    w_down,
    w_up,
):
    section = lax.axis_index("pipe")
    is_last = section == lax.axis_size("pipe") - 1
    count = lax.axis_size("dp")
    chips = count // 2
    gain = norm_gain
    first, stash, grad = act_in[0, 0], stash_a[0, 0], grad_in[0, 0]
    down, up = w_down[0], w_up[0]
    rows, full = first.shape
    rank, width = up.shape
    sent_to, kept_by = targets()
    scalars = jnp.stack(
        [is_last.astype(jnp.int32), (section == 0).astype(jnp.int32)]
        + owners() + sent_to + kept_by
    ).astype(jnp.int32)

    def vmem(dims):
        return pltpu.VMEM(dims, BF16)

    act, ups_shape, downs_shape = (rows, full), (count, rank, width), (count, width, rank)

    down_far = far_pieces(down)
    text_arrays, text_early, text_waiting, order = tree_start([text_emb])
    _, map_came = tree_round([w_vision], 2)
    down_near, up_near = swap_cores(down), swap_cores(up)
    prep_outs = [shape(act, BF16), shape((rows, 128), F32)]
    normed_a, scale_a = call(prep_kernel, scalars, [first, gain], prep_outs)
    normed_s, scale_s = call(prep_kernel, scalars, [stash, gain], prep_outs)
    up = tied(up, normed_a, normed_s, *down_far)
    up_far = far_pieces(up)
    downs = with_far(down, down_near, down_far)

    inner_a, out_own = call(
        functools.partial(forward_kernel, count), scalars, [normed_a, first, up] + downs,
        [shape((rows, rank), F32), shape((rows, width), BF16)],
        in_specs={1: pl.BlockSpec((rows, width), lambda i, s: (0, s[2]))},
    )
    came_own = passed_along(out_own, 1)
    text_arrays += [text_early, to_first(tied(text_waiting, out_own))]
    (inner_s,) = call(
        functools.partial(inner_kernel, count), scalars, [tied(normed_s, out_own)] + downs,
        [shape((rows, rank), F32)],
    )
    query = tied(enc_query[0], out_own)
    attended = encode_section(query, enc_key[0], enc_value[0])

    ups = with_far(up, up_near, up_far)
    back_scratch = [vmem(act)] * 3 + [
        vmem(ups_shape), vmem(downs_shape), pltpu.SemaphoreType.DMA((2 + 3 * count,))
    ]
    hands = set(range(5, 5 + 2 * count)) | {0, 1}
    back0, factor0 = call(
        functools.partial(back_kernel, count, False), scalars,
        [tied(stash, came_own, attended, map_came, *text_arrays[1:]), grad, inner_s, scale_s, gain] + ups + downs,
        [shape(act, BF16), shape((rows, rank), BF16)],
        scratch=back_scratch, by_hand=hands, outs_by_hand={0},
    )
    after = passed_along(back0, -1)

    groups = [1, count - 2]
    rests = call(
        functools.partial(rest_kernel, count - 1), scalars,
        [tied(first, factor0), inner_a] + ups[1:], [shape((rows, group * width), BF16) for group in groups],
    )
    merge_own = tied(w_merge, factor0).T
    merge_pieces = direct_pieces(merge_own)

    tokens = tokens_of(attended, merge_gain, merge_pieces, tok_count, tok_offset)

    after = tied(after, tokens, *rests)
    came_rests, before = [], after
    for rest in rests:
        before = passed_along(tied(rest, before), 1)
        came_rests.append(before)
    map_arrays, map_early, map_waiting, _ = tree_start([w_vision[None], tied(map_came, after)], 4)
    map_arrays += [map_early, to_first(map_waiting)]

    ups_out = [shape((rank, width), BF16)] * chips + [shape((rank, width), F32)] * chips
    downs_out = [shape((width, rank), BF16)] * chips + [shape((width, rank), F32)] * chips
    factor1, *slices = call(
        functools.partial(terms_kernel, count), scalars,
        [stash, first, grad, after, inner_s, inner_a, factor0, scale_s, scale_a, gain] + ups,
        [shape((rows, rank), BF16)] + ups_out + downs_out,
        scratch=[
            vmem((2 * rows, full)), vmem(act), vmem(act), vmem(ups_shape),
            pltpu.SemaphoreType.DMA((4 + count,)),
        ],
        by_hand={0, 1, 2, 3} | set(range(10, 10 + count)), room=58,
    )
    up_slices, down_slices = slices[:count], slices[count:]
    sums = []
    for slices in (up_slices, down_slices):
        sent, kept = slices[:chips], slices[chips:]
        terms = [kept[0] + swap_cores(sent[0]).astype(F32)]
        for k in range(chips - 1, 0, -1):
            far = (kept[k] + swap_cores(sent[k]).astype(F32)).astype(BF16)
            terms.append(shift_chips(far, k))
        sums.append(terms)
    token_arrays, token_early, token_waiting, _ = tree_start([tied(tokens, after)[None]])
    (back1,) = call(
        functools.partial(back_kernel, count, True), scalars,
        [first, after, inner_a, scale_a, gain, factor1] + ups + downs,
        [shape(act, BF16)],
        scratch=back_scratch, by_hand=set(range(6, 6 + 2 * count)) | {0, 1}, outs_by_hand={0},
    )

    token_arrays += [token_early, to_first(token_waiting)]
    n_arrays, n_pipe = len(token_arrays), lax.axis_size("pipe")
    blocks_at = 2 + len(came_rests)
    (out1,) = call(
        functools.partial(last_kernel, count, order, n_arrays), scalars,
        [gain, came_own] + came_rests + token_arrays + text_arrays + map_arrays + downs + ups, [shape(act, BF16)],
        scratch=[vmem(act)] * 2 + [
            vmem(ups_shape), vmem(downs_shape), vmem((2, n_pipe) + w_vision.shape),
            pltpu.SemaphoreType.DMA((4 * count,)), pltpu.SemaphoreType.DMA((2, n_pipe)),
        ],
        by_hand=set(range(1, blocks_at)) | set(range(blocks_at + n_arrays, blocks_at + 3 * n_arrays + 2 * count)), outs_by_hand={0},
        room=18,
    )
    grad_up, grad_down = (
        sum((tied(term, out1).astype(F32) for term in terms[1:]), terms[0]) for terms in sums
    )
    return (out1[None, None], back1[None, None], grad_down[None], grad_up[None])


def solution(mesh):
    in_specs = (
        P("dp", "pipe", None, None),
        P("dp", "pipe", None, None),
        P("dp", "pipe", None, None),
        P("dp", None, "pipe"),
        P("dp", "pipe", None),
        P("dp", "pipe", None),
        P("dp", "pipe", None),
        P("dp", "pipe"),
        P("dp", "pipe"),
        P(),
        P(None, "dp"),
        P(None, "pipe"),
        P("pipe", None),
        P("pipe", "dp", None),
        P("pipe", None, "dp"),
    )
    out_specs = (
        P("dp", "pipe", None, None),
        P("dp", "pipe", None, None),
        P("pipe", "dp", None),
        P("pipe", None, "dp"),
    )
    return jax.shard_map(body, mesh=mesh, in_specs=in_specs, out_specs=out_specs, check_vma=False)
```

```python
import functools

import jax
import jax.numpy as jnp
from jax import lax
from jax.experimental import pallas as pl
from jax.experimental.pallas import tpu as pltpu
from jax.sharding import PartitionSpec as P

HEADS = 25
HEAD_DIM = 128
EPS = 1e-06
F32 = jnp.float32
BF16 = jnp.bfloat16
MIB = 1 << 20


def dot(a, b):
    return jnp.dot(a, b, preferred_element_type=F32)


def dot_nt(a, b):
    return lax.dot_general(a, b, (((1,), (1,)), ((), ())), preferred_element_type=F32)


def dot_tn(a, b):
    return lax.dot_general(a, b, (((0,), (0,)), ((), ())), preferred_element_type=F32)


def swap_cores(array):
    count = lax.axis_size("dp")
    return lax.ppermute(array, "dp", [(i, i ^ 1) for i in range(count)])


def shift_chips(array, by):
    count = lax.axis_size("dp")
    return lax.ppermute(array, "dp", [(i, (i + 2 * by) % count) for i in range(count)])


def tied(array, *others):
    return lax.optimization_barrier((array,) + others)[0]


def owners():
    me = lax.axis_index("dp")
    chips = lax.axis_size("dp") // 2
    chip, core = me // 2, me % 2
    out = []
    for k in range(chips):
        behind = lax.rem(chip - k + chips, chips)
        out += [behind * 2 + core, behind * 2 + 1 - core]
    return out


def targets():
    me = lax.axis_index("dp")
    chips = lax.axis_size("dp") // 2
    chip, core = me // 2, me % 2
    aheads = [lax.rem(chip + k, chips) for k in range(chips)]
    return [a * 2 + 1 - core for a in aheads], [a * 2 + core for a in aheads]


def far_pieces(shard):
    chips = lax.axis_size("dp") // 2
    return [shift_chips(shard, k) for k in range(1, chips)]


def with_far(shard, near, far):
    out = [shard, near]
    for piece in far:
        out += [piece, swap_cores(piece)]
    return out


def direct_pieces(shard):
    length = lax.axis_size("dp")
    out = [shard, swap_cores(shard)]
    for k in range(1, length // 2):
        pairs = [(i, ((i + 2 * k) % length) ^ 1) for i in range(length)]
        out += [shift_chips(shard, k), lax.ppermute(shard, "dp", pairs)]
    return out


def passed_along(array, by):
    length = lax.axis_size("pipe")
    pairs = [(i, i + by) for i in range(length) if 0 <= i + by < length]
    return lax.ppermute(array, "pipe", pairs)


def columns(index, size):
    return pl.ds(pl.multiple_of(index * size, size), size)


def chunk_of(width):
    return min(width, 512)


def call(kernel, scalars, ins, outs, scratch=(), in_specs=None, by_hand=(), outs_by_hand=(), cost=1, room=14):
    def whole(shape):
        return pl.BlockSpec(shape, lambda i, s, n=len(shape): (0,) * n)

    anywhere = pl.BlockSpec(memory_space=pl.ANY)
    specs = [anywhere if at in by_hand else whole(a.shape) for at, a in enumerate(ins)]
    for at, spec in (in_specs or {}).items():
        specs[at] = spec
    return pl.pallas_call(
        kernel,
        grid_spec=pltpu.PrefetchScalarGridSpec(
            num_scalar_prefetch=1,
            grid=(1,),
            in_specs=specs,
            out_specs=[anywhere if at in outs_by_hand else whole(o.shape) for at, o in enumerate(outs)],
            scratch_shapes=list(scratch),
        ),
        out_shape=list(outs),
        compiler_params=pltpu.CompilerParams(vmem_limit_bytes=room * MIB),
        cost_estimate=pl.CostEstimate(flops=cost, bytes_accessed=1, transcendentals=0),
    )(scalars, *ins)


def shape(dims, dtype):
    return jax.ShapeDtypeStruct(dims, dtype)


def started(source, target, sem):
    copy = pltpu.make_async_copy(source, target, sem)
    copy.start()
    return copy


def hidden_of(inner):
    return (inner * jax.nn.sigmoid(inner)).astype(BF16)


def factor_of(inner, back_h):
    sig = jax.nn.sigmoid(inner)
    return (back_h * sig * (1.0 + inner * (1.0 - sig))).astype(BF16)


def scale_into(x_ref, width):
    size = chunk_of(width)

    def add(j, acc):
        x = x_ref[:, columns(j, size)].astype(F32)
        return acc + x * x

    total = lax.fori_loop(0, width // size, add, jnp.zeros((x_ref.shape[0], size), F32))
    return lax.rsqrt(jnp.sum(total, -1, keepdims=True) / width + EPS)


def prep_kernel(s_ref, x_ref, gain_ref, normed_ref, scale_ref):
    rows, width = x_ref.shape
    size = chunk_of(width)
    scale = scale_into(x_ref, width)
    scale_ref[...] = jnp.broadcast_to(scale, (rows, 128))

    def write(j, carry):
        cols = columns(j, size)
        x = x_ref[:, cols].astype(F32)
        normed_ref[:, cols] = (x * scale * gain_ref[:, cols]).astype(BF16)
        return carry

    lax.fori_loop(0, width // size, write, 0)


def inner_from(s_ref, normed_ref, downs):
    width = downs[0].shape[0]
    inner = dot(normed_ref[:, columns(s_ref[2], width)], downs[0][...])
    for k in range(1, len(downs)):
        inner += dot(normed_ref[:, columns(s_ref[2 + k], width)], downs[k][...])
    return inner


def inner_kernel(count, s_ref, normed_ref, *refs):
    refs[count][...] = inner_from(s_ref, normed_ref, refs[:count])


def forward_kernel(count, s_ref, normed_ref, first_own_ref, up_own_ref, *refs):
    downs, (inner_ref, out_ref) = refs[:count], refs[count:]
    width = downs[0].shape[0]
    inner = inner_from(s_ref, normed_ref, downs)
    inner_ref[...] = inner
    hidden = hidden_of(inner)
    size = chunk_of(width)
    for j in range(width // size):
        cols = pl.ds(j * size, size)
        x = first_own_ref[:, cols].astype(F32)
        out_ref[:, cols] = (x + dot(hidden, up_own_ref[:, cols])).astype(BF16)


def forward_into(s_ref, x_ref, hidden, up, out_ref, rows):
    count, _, width = up.shape
    size = chunk_of(width)
    for k in range(count):
        for j in range(width // size):
            cols = pl.ds(pl.multiple_of(s_ref[2 + k] * width + j * size, size), size)
            x = x_ref[:, cols].astype(F32)
            out_ref[rows, cols] = (x + dot(hidden, up[k, :, pl.ds(j * size, size)])).astype(BF16)


def factor_from(s_ref, grad_ref, rows, inner, up):
    count, _, width = up.shape
    back_h = dot_nt(grad_ref[rows, columns(s_ref[2], width)], up[0])
    for k in range(1, count):
        back_h += dot_nt(grad_ref[rows, columns(s_ref[2 + k], width)], up[k])
    return factor_of(inner, back_h)


def back_kernel(count, given, s_ref, x_hbm, came_hbm, inner_ref, scale_ref, gain_ref, *refs):
    refs = list(refs)
    factor_in = refs.pop(0) if given else None
    ups, downs, refs = refs[:count], refs[count:2 * count], refs[2 * count:]
    out_hbm = refs.pop(0)
    factor_out = None if given else refs.pop(0)
    x_ref, grad_ref, out_ref, up, down, sems = refs
    rows, full = x_ref.shape
    width = up.shape[2]
    size = chunk_of(width)
    every = pl.ds(0, rows)
    is_last = s_ref[0] == 1
    grad_copy = started(came_hbm, grad_ref, sems.at[0])

    def load_ups():
        return [started(ups[k], up.at[k], sems.at[2 + k]) for k in range(count)]

    up_copies = [] if given else load_ups()
    x_copy = started(x_hbm, x_ref, sems.at[1])
    down_copies = [started(downs[k], down.at[k], sems.at[2 + count + k]) for k in range(count)]
    inner = inner_ref[...]
    grad_copy.wait()
    for copy in up_copies:
        copy.wait()
    if given:
        x_copy.wait()

    @pl.when(is_last)
    def _():
        if given:
            for copy in load_ups():
                copy.wait()
        else:
            x_copy.wait()
        forward_into(s_ref, x_ref, hidden_of(inner), up, grad_ref, every)

    if given:
        factor = factor_in[...]
    else:
        factor = factor_from(s_ref, grad_ref, every, inner, up)
        factor_out[...] = factor

        @pl.when(jnp.logical_not(is_last))
        def _():
            x_copy.wait()

    mean = jnp.sum(factor.astype(F32) * inner, -1, keepdims=True) / full
    scale = scale_ref[:, 0:1]
    bend = scale * scale * mean
    out_copies = []
    for k in range(count):
        down_copies[k].wait()
        for j in range(width // size):
            cols = pl.ds(pl.multiple_of(s_ref[2 + k] * width + j * size, size), size)
            back_n = dot_nt(factor, down[k, pl.ds(j * size, size), :]) * gain_ref[:, cols]
            x = x_ref[:, cols].astype(F32)
            grad = grad_ref[:, cols].astype(F32)
            out_ref[:, cols] = (grad + (scale * back_n - bend * x)).astype(BF16)
        cols = columns(s_ref[2 + k], width)
        out_copies.append(
            started(out_ref.at[:, cols], out_hbm.at[:, cols], sems.at[2 + 2 * count + k])
        )
    for copy in out_copies:
        copy.wait()


def rest_kernel(count, s_ref, first_ref, inner_ref, *refs):
    ups, out_refs = refs[:count], refs[count:]
    width = ups[0].shape[1]
    size = chunk_of(width)
    hidden = hidden_of(inner_ref[...])
    places = [(ref, at) for ref in out_refs for at in range(ref.shape[1] // width)]
    for k, (out_ref, at) in enumerate(places):
        for j in range(width // size):
            cols = pl.ds(pl.multiple_of(s_ref[3 + k] * width + j * size, size), size)
            x = first_ref[:, cols].astype(F32)
            out_ref[:, pl.ds(at * width + j * size, size)] = (
                x + dot(hidden, ups[k][:, pl.ds(j * size, size)])
            ).astype(BF16)


def terms_kernel(
    count, s_ref, stash_hbm, first_hbm, came0_hbm, came1_hbm, inner_s_ref, inner_a_ref,
    factor0_ref, scale_s_ref, scale_a_ref, gain_ref, *refs
):
    ups, refs = refs[:count], refs[count:]
    factor_ref, up_slices, down_slices = refs[0], refs[1:1 + count], refs[1 + count:1 + 2 * count]
    grads, x_s, x_a, up, sems = refs[1 + 2 * count:]
    rows, _ = x_s.shape
    width = up.shape[2]
    size = chunk_of(width)
    first_rows, second_rows = pl.ds(0, rows), pl.ds(rows, rows)
    copies = [started(came1_hbm, grads.at[second_rows], sems.at[0])]
    copies += [started(ups[k], up.at[k], sems.at[4 + k]) for k in range(count)]
    copies += [started(came0_hbm, grads.at[first_rows], sems.at[1])]
    late = [started(stash_hbm, x_s, sems.at[2]), started(first_hbm, x_a, sems.at[3])]
    hidden_s, hidden_a = hidden_of(inner_s_ref[...]), hidden_of(inner_a_ref[...])
    for copy in copies:
        copy.wait()

    @pl.when(s_ref[0] == 1)
    def _():
        for copy in late:
            copy.wait()
        forward_into(s_ref, x_s, hidden_s, up, grads, first_rows)
        forward_into(s_ref, x_a, hidden_a, up, grads, second_rows)

    factor1 = factor_from(s_ref, grads, second_rows, inner_a_ref[...], up)
    factor_ref[...] = factor1
    hidden = jnp.concatenate([hidden_s, hidden_a], 0).astype(F32).T.astype(BF16)
    for k, ref in enumerate(up_slices):
        base = s_ref[2 + count + k] * width
        for j in range(width // size):
            cols = pl.ds(pl.multiple_of(base + j * size, size), size)
            ref[:, pl.ds(j * size, size)] = dot(hidden, grads[:, cols]).astype(ref.dtype)
    factor = jnp.concatenate([factor0_ref[...], factor1], 0)

    @pl.when(s_ref[0] == 0)
    def _():
        for copy in late:
            copy.wait()

    pairs = ((x_s, scale_s_ref[:, 0:1]), (x_a, scale_a_ref[:, 0:1]))
    for k, ref in enumerate(down_slices):
        base = s_ref[2 + count + k] * width
        for j in range(width // size):
            cols = pl.ds(pl.multiple_of(base + j * size, size), size)
            normed = jnp.concatenate(
                [(x[:, cols].astype(F32) * scale * gain_ref[:, cols]).astype(BF16) for x, scale in pairs], 0
            )
            ref[pl.ds(j * size, size), :] = dot_tn(normed, factor).astype(ref.dtype)


def compose_into(x_ref, order, blocks, texts, maps, part_ref, sems):
    rows, _ = x_ref.shape
    size = part_ref.shape[3]
    copies = []
    for half, refs in enumerate((texts, maps)):
        slabs = [(ref, k) for ref in refs for k in range(ref.shape[0])]
        for at, (ref, k) in enumerate(slabs):
            copies.append(started(ref.at[k], part_ref.at[half, at], sems.at[half, at]))
    flat = [ref[k].astype(F32) for ref in blocks for k in range(ref.shape[0])]
    slots = flat[0].shape[0] // 2
    row = lax.broadcasted_iota(jnp.int32, (rows, slots), 0).astype(F32)
    slot = lax.broadcasted_iota(jnp.int32, (rows, slots), 1).astype(F32)
    vision = jnp.zeros((rows, flat[0].shape[1]), F32)
    marked = jnp.zeros((rows, 1), F32)
    for block in flat:
        number, first_row = block[slots:slots + 1, 0:1], block[slots:slots + 1, 1:2]
        placed = jnp.where((row == first_row + slot) & (slot < number), 1.0, 0.0)
        vision += dot(placed.astype(BF16), block[:slots].astype(BF16))
        marked += jnp.sum(placed, -1, keepdims=True)
    vision = vision.astype(BF16)
    for at, section in enumerate(order):
        copies[at].wait()
        copies[len(order) + at].wait()
        mapped = dot(vision, part_ref[1, at])
        text = part_ref[0, at].astype(F32)
        x_ref[:, pl.ds(section * size, size)] = jnp.where(marked > 0.5, mapped, text).astype(BF16)


def last_kernel(count, order, n_arrays, s_ref, gain_ref, own_hbm, *refs):
    refs = list(refs)
    rests, refs = refs[:2], refs[2:]
    blocks, texts, maps = (refs[at * n_arrays:(at + 1) * n_arrays] for at in range(3))
    refs = refs[3 * n_arrays:]
    downs, ups = refs[:count], refs[count:2 * count]
    out_hbm, x_ref, out_ref, up, down, part_ref, sems, part_sems = refs[2 * count:]
    width = up.shape[2]
    rows, full = x_ref.shape
    size = chunk_of(width)

    @pl.when(s_ref[1] == 1)
    def _():
        compose_into(x_ref, order, blocks, texts, maps, part_ref, part_sems)

    @pl.when(s_ref[1] == 0)
    def _():
        copies = [started(own_hbm, x_ref.at[:, columns(s_ref[2], width)], sems.at[0])]
        for ref in rests:
            for at in range(ref.shape[1] // width):
                k = len(copies)
                copies.append(
                    started(
                        ref.at[:, pl.ds(at * width, width)],
                        x_ref.at[:, columns(s_ref[2 + k], width)],
                        sems.at[k],
                    )
                )
        for copy in copies:
            copy.wait()

    down_copies = [started(downs[k], down.at[k], sems.at[count + k]) for k in range(count)]
    up_copies = [started(ups[k], up.at[k], sems.at[2 * count + k]) for k in range(count)]
    scale = scale_into(x_ref, full)
    inner = jnp.zeros((rows, down.shape[2]), F32)
    for k in range(count):
        down_copies[k].wait()
        for j in range(width // size):
            cols = pl.ds(pl.multiple_of(s_ref[2 + k] * width + j * size, size), size)
            normed = (x_ref[:, cols].astype(F32) * scale * gain_ref[:, cols]).astype(BF16)
            inner += dot(normed, down[k, pl.ds(j * size, size), :])
    hidden = hidden_of(inner)
    out_copies = []
    for k in range(count):
        up_copies[k].wait()
        for j in range(width // size):
            cols = pl.ds(pl.multiple_of(s_ref[2 + k] * width + j * size, size), size)
            x = x_ref[:, cols].astype(F32)
            out_ref[:, cols] = (x + dot(hidden, up[k, :, pl.ds(j * size, size)])).astype(BF16)
        cols = columns(s_ref[2 + k], width)
        out_copies.append(
            started(out_ref.at[:, cols], out_hbm.at[:, cols], sems.at[3 * count + k])
        )
    for copy in out_copies:
        copy.wait()


def encode_section(query, keys, values):
    q3 = query.reshape(query.shape[0], HEADS, HEAD_DIM)
    k3 = keys.reshape(keys.shape[0], HEADS, HEAD_DIM)
    v3 = values.reshape(values.shape[0], HEADS, HEAD_DIM)
    scores = jnp.einsum("qhd,khd->hqk", q3, k3, preferred_element_type=F32) * HEAD_DIM ** (-0.5)
    top = jnp.max(scores, -1, keepdims=True)
    weights = jnp.exp(scores - top)
    probs = (weights / jnp.sum(weights, -1, keepdims=True)).astype(BF16)
    attended = jnp.einsum("hqk,khd->qhd", probs, v3, preferred_element_type=F32)
    return attended.reshape(query.shape[0], HEADS * HEAD_DIM).astype(BF16)


def tree_round(held, step):
    length = lax.axis_size("pipe")
    pairs = [(i + at + step, i + at) for i in range(0, length, 2 * step) for at in (0, 1)]
    packed = jnp.stack(held)
    return packed, lax.ppermute(packed, "pipe", pairs)


def tree_start(arrays, step=2):
    length = lax.axis_size("pipe")
    arrays = list(arrays)
    while step < length:
        packed, came = tree_round([a[k] for a in arrays for k in range(a.shape[0])], step)
        if 2 * step == length:
            early = to_first(packed)
        arrays.append(came)
        step *= 2
    order = [0]
    for at in range(1, length.bit_length() - 1):
        order = order + [section + 2**at for section in order]
    return arrays, early, came, order + [section + 1 for section in order]


def to_first(array):
    return lax.ppermute(array, "pipe", [(1, 0)])


def tokens_of(attended, merge_gain, merge_pieces, tok_count, tok_offset):
    slots = attended.shape[0]
    x32 = attended.astype(F32)
    scale = lax.rsqrt(jnp.mean(x32 * x32, -1, keepdims=True) + EPS)
    normed = (x32 * scale * merge_gain).astype(BF16)
    merged = [jax.nn.gelu(dot_nt(normed, piece)).astype(BF16) for piece in merge_pieces]
    size = merged[0].shape[1]
    tokens = jnp.zeros((slots, size * len(merged)), BF16)
    for piece, owner in zip(merged, owners()):
        tokens = lax.dynamic_update_slice_in_dim(tokens, piece, owner * size, 1)
    place = jnp.concatenate([tok_count, tok_offset], 1).astype(BF16)
    place = jnp.pad(place, ((0, slots - 1), (0, tokens.shape[1] - 2)))
    return jnp.concatenate([tokens, place], 0)


def body(
    act_in,
    stash_a,
    grad_in,
    text_emb,
    enc_query,
    enc_key,
    enc_value,
    tok_count,
    tok_offset,
    merge_gain,
    w_merge,
    w_vision,
    norm_gain,
    w_down,
    w_up,
):
    section = lax.axis_index("pipe")
    is_last = section == lax.axis_size("pipe") - 1
    count = lax.axis_size("dp")
    chips = count // 2
    gain = norm_gain
    first, stash, grad = act_in[0, 0], stash_a[0, 0], grad_in[0, 0]
    down, up = w_down[0], w_up[0]
    rows, full = first.shape
    rank, width = up.shape
    sent_to, kept_by = targets()
    scalars = jnp.stack(
        [is_last.astype(jnp.int32), (section == 0).astype(jnp.int32)]
        + owners() + sent_to + kept_by
    ).astype(jnp.int32)

    def vmem(dims):
        return pltpu.VMEM(dims, BF16)

    act, ups_shape, downs_shape = (rows, full), (count, rank, width), (count, width, rank)

    down_far = far_pieces(down)
    text_arrays, text_early, text_waiting, order = tree_start([text_emb])
    _, map_came = tree_round([w_vision], 2)
    down_near, up_near = swap_cores(down), swap_cores(up)
    prep_outs = [shape(act, BF16), shape((rows, 128), F32)]
    normed_a, scale_a = call(prep_kernel, scalars, [first, gain], prep_outs)
    normed_s, scale_s = call(prep_kernel, scalars, [stash, gain], prep_outs)
    up = tied(up, normed_a, normed_s, *down_far)
    up_far = far_pieces(up)
    downs = with_far(down, down_near, down_far)

    inner_a, out_own = call(
        functools.partial(forward_kernel, count), scalars, [normed_a, first, up] + downs,
        [shape((rows, rank), F32), shape((rows, width), BF16)],
        in_specs={1: pl.BlockSpec((rows, width), lambda i, s: (0, s[2]))},
    )
    came_own = passed_along(out_own, 1)
    text_arrays += [text_early, to_first(tied(text_waiting, out_own, text_early))]
    (inner_s,) = call(
        functools.partial(inner_kernel, count), scalars, [tied(normed_s, out_own)] + downs,
        [shape((rows, rank), F32)],
    )
    query = tied(enc_query[0], out_own)
    attended = encode_section(query, enc_key[0], enc_value[0])

    ups = with_far(up, up_near, up_far)
    back_scratch = [vmem(act)] * 3 + [
        vmem(ups_shape), vmem(downs_shape), pltpu.SemaphoreType.DMA((2 + 3 * count,))
    ]
    hands = set(range(5, 5 + 2 * count)) | {0, 1}
    back0, factor0 = call(
        functools.partial(back_kernel, count, False), scalars,
        [tied(stash, came_own, attended, map_came, *text_arrays[1:]), grad, inner_s, scale_s, gain] + ups + downs,
        [shape(act, BF16), shape((rows, rank), BF16)],
        scratch=back_scratch, by_hand=hands, outs_by_hand={0},
    )
    after = passed_along(back0, -1)

    groups = [1, count - 2]
    rests = call(
        functools.partial(rest_kernel, count - 1), scalars,
        [tied(first, factor0), inner_a] + ups[1:], [shape((rows, group * width), BF16) for group in groups],
    )
    merge_own = tied(w_merge, factor0).T
    merge_pieces = direct_pieces(merge_own)

    tokens = tokens_of(attended, merge_gain, merge_pieces, tok_count, tok_offset)

    after = tied(after, tokens, *rests)
    came_rests, before = [], after
    for rest in rests:
        before = passed_along(tied(rest, before), 1)
        came_rests.append(before)
    map_arrays, map_early, map_waiting, _ = tree_start([w_vision[None], tied(map_came, after)], 4)
    map_arrays += [map_early, to_first(map_waiting)]

    ups_out = [shape((rank, width), BF16)] * chips + [shape((rank, width), F32)] * chips
    downs_out = [shape((width, rank), BF16)] * chips + [shape((width, rank), F32)] * chips
    factor1, *slices = call(
        functools.partial(terms_kernel, count), scalars,
        [stash, first, grad, after, inner_s, inner_a, factor0, scale_s, scale_a, gain] + ups,
        [shape((rows, rank), BF16)] + ups_out + downs_out,
        scratch=[
            vmem((2 * rows, full)), vmem(act), vmem(act), vmem(ups_shape),
            pltpu.SemaphoreType.DMA((4 + count,)),
        ],
        by_hand={0, 1, 2, 3} | set(range(10, 10 + count)), room=58,
    )
    up_slices, down_slices = slices[:count], slices[count:]
    sums = []
    for slices in (up_slices, down_slices):
        sent, kept = slices[:chips], slices[chips:]
        terms = [kept[0] + swap_cores(sent[0]).astype(F32)]
        for k in range(chips - 1, 0, -1):
            far = (kept[k] + swap_cores(sent[k]).astype(F32)).astype(BF16)
            terms.append(shift_chips(far, k))
        sums.append(terms)
    token_arrays, token_early, token_waiting, _ = tree_start([tied(tokens, after)[None]])
    (back1,) = call(
        functools.partial(back_kernel, count, True), scalars,
        [first, after, inner_a, scale_a, gain, factor1] + ups + downs,
        [shape(act, BF16)],
        scratch=back_scratch, by_hand=set(range(6, 6 + 2 * count)) | {0, 1}, outs_by_hand={0},
    )

    token_arrays += [token_early, to_first(token_waiting)]
    n_arrays, n_pipe = len(token_arrays), lax.axis_size("pipe")
    blocks_at = 2 + len(came_rests)
    (out1,) = call(
        functools.partial(last_kernel, count, order, n_arrays), scalars,
        [gain, came_own] + came_rests + token_arrays + text_arrays + map_arrays + downs + ups, [shape(act, BF16)],
        scratch=[vmem(act)] * 2 + [
            vmem(ups_shape), vmem(downs_shape), vmem((2, n_pipe) + w_vision.shape),
            pltpu.SemaphoreType.DMA((4 * count,)), pltpu.SemaphoreType.DMA((2, n_pipe)),
        ],
        by_hand=set(range(1, blocks_at)) | set(range(blocks_at + n_arrays, blocks_at + 3 * n_arrays + 2 * count)), outs_by_hand={0},
        room=18,
    )
    grad_up, grad_down = (
        sum((tied(term, out1).astype(F32) for term in terms[1:]), terms[0]) for terms in sums
    )
    return (out1[None, None], back1[None, None], grad_down[None], grad_up[None])


def solution(mesh):
    in_specs = (
        P("dp", "pipe", None, None),
        P("dp", "pipe", None, None),
        P("dp", "pipe", None, None),
        P("dp", None, "pipe"),
        P("dp", "pipe", None),
        P("dp", "pipe", None),
        P("dp", "pipe", None),
        P("dp", "pipe"),
        P("dp", "pipe"),
        P(),
        P(None, "dp"),
        P(None, "pipe"),
        P("pipe", None),
        P("pipe", "dp", None),
        P("pipe", None, "dp"),
    )
    out_specs = (
        P("dp", "pipe", None, None),
        P("dp", "pipe", None, None),
        P("pipe", "dp", None),
        P("pipe", None, "dp"),
    )
    return jax.shard_map(body, mesh=mesh, in_specs=in_specs, out_specs=out_specs, check_vma=False)
```

```python
import functools

import jax
import jax.numpy as jnp
from jax import lax
from jax.experimental import pallas as pl
from jax.experimental.pallas import tpu as pltpu
from jax.sharding import PartitionSpec as P

HEADS = 25
HEAD_DIM = 128
EPS = 1e-06
F32 = jnp.float32
BF16 = jnp.bfloat16
MIB = 1 << 20


def dot(a, b):
    return jnp.dot(a, b, preferred_element_type=F32)


def dot_nt(a, b):
    return lax.dot_general(a, b, (((1,), (1,)), ((), ())), preferred_element_type=F32)


def dot_tn(a, b):
    return lax.dot_general(a, b, (((0,), (0,)), ((), ())), preferred_element_type=F32)


def swap_cores(array):
    count = lax.axis_size("dp")
    return lax.ppermute(array, "dp", [(i, i ^ 1) for i in range(count)])


def shift_chips(array, by):
    count = lax.axis_size("dp")
    return lax.ppermute(array, "dp", [(i, (i + 2 * by) % count) for i in range(count)])


def tied(array, *others):
    return lax.optimization_barrier((array,) + others)[0]


def owners():
    me = lax.axis_index("dp")
    chips = lax.axis_size("dp") // 2
    chip, core = me // 2, me % 2
    out = []
    for k in range(chips):
        behind = lax.rem(chip - k + chips, chips)
        out += [behind * 2 + core, behind * 2 + 1 - core]
    return out


def targets():
    me = lax.axis_index("dp")
    chips = lax.axis_size("dp") // 2
    chip, core = me // 2, me % 2
    aheads = [lax.rem(chip + k, chips) for k in range(chips)]
    return [a * 2 + 1 - core for a in aheads], [a * 2 + core for a in aheads]


def far_pieces(shard):
    chips = lax.axis_size("dp") // 2
    return [shift_chips(shard, k) for k in range(1, chips)]


def with_far(shard, near, far):
    out = [shard, near]
    for piece in far:
        out += [piece, swap_cores(piece)]
    return out


def direct_pieces(shard):
    length = lax.axis_size("dp")
    out = [shard, swap_cores(shard)]
    for k in range(1, length // 2):
        pairs = [(i, ((i + 2 * k) % length) ^ 1) for i in range(length)]
        out += [shift_chips(shard, k), lax.ppermute(shard, "dp", pairs)]
    return out


def passed_along(array, by):
    length = lax.axis_size("pipe")
    pairs = [(i, i + by) for i in range(length) if 0 <= i + by < length]
    return lax.ppermute(array, "pipe", pairs)


def columns(index, size):
    return pl.ds(pl.multiple_of(index * size, size), size)


def chunk_of(width):
    return min(width, 512)


def call(kernel, scalars, ins, outs, scratch=(), in_specs=None, by_hand=(), outs_by_hand=(), cost=1, room=14):
    def whole(shape):
        return pl.BlockSpec(shape, lambda i, s, n=len(shape): (0,) * n)

    anywhere = pl.BlockSpec(memory_space=pl.ANY)
    specs = [anywhere if at in by_hand else whole(a.shape) for at, a in enumerate(ins)]
    for at, spec in (in_specs or {}).items():
        specs[at] = spec
    return pl.pallas_call(
        kernel,
        grid_spec=pltpu.PrefetchScalarGridSpec(
            num_scalar_prefetch=1,
            grid=(1,),
            in_specs=specs,
            out_specs=[anywhere if at in outs_by_hand else whole(o.shape) for at, o in enumerate(outs)],
            scratch_shapes=list(scratch),
        ),
        out_shape=list(outs),
        compiler_params=pltpu.CompilerParams(vmem_limit_bytes=room * MIB),
        cost_estimate=pl.CostEstimate(flops=cost, bytes_accessed=1, transcendentals=0),
    )(scalars, *ins)


def shape(dims, dtype):
    return jax.ShapeDtypeStruct(dims, dtype)


def started(source, target, sem):
    copy = pltpu.make_async_copy(source, target, sem)
    copy.start()
    return copy


def hidden_of(inner):
    return (inner * jax.nn.sigmoid(inner)).astype(BF16)


def factor_of(inner, back_h):
    sig = jax.nn.sigmoid(inner)
    return (back_h * sig * (1.0 + inner * (1.0 - sig))).astype(BF16)


def scale_into(x_ref, width):
    size = chunk_of(width)

    def add(j, acc):
        x = x_ref[:, columns(j, size)].astype(F32)
        return acc + x * x

    total = lax.fori_loop(0, width // size, add, jnp.zeros((x_ref.shape[0], size), F32))
    return lax.rsqrt(jnp.sum(total, -1, keepdims=True) / width + EPS)


def prep_kernel(s_ref, x_ref, gain_ref, normed_ref, scale_ref):
    rows, width = x_ref.shape
    size = chunk_of(width)
    scale = scale_into(x_ref, width)
    scale_ref[...] = jnp.broadcast_to(scale, (rows, 128))

    def write(j, carry):
        cols = columns(j, size)
        x = x_ref[:, cols].astype(F32)
        normed_ref[:, cols] = (x * scale * gain_ref[:, cols]).astype(BF16)
        return carry

    lax.fori_loop(0, width // size, write, 0)


def inner_from(s_ref, normed_ref, downs):
    width = downs[0].shape[0]
    inner = dot(normed_ref[:, columns(s_ref[2], width)], downs[0][...])
    for k in range(1, len(downs)):
        inner += dot(normed_ref[:, columns(s_ref[2 + k], width)], downs[k][...])
    return inner


def inner_kernel(count, s_ref, normed_ref, *refs):
    refs[count][...] = inner_from(s_ref, normed_ref, refs[:count])


def forward_kernel(count, s_ref, normed_ref, first_own_ref, up_own_ref, *refs):
    downs, (inner_ref, out_ref) = refs[:count], refs[count:]
    width = downs[0].shape[0]
    inner = inner_from(s_ref, normed_ref, downs)
    inner_ref[...] = inner
    hidden = hidden_of(inner)
    size = chunk_of(width)
    for j in range(width // size):
        cols = pl.ds(j * size, size)
        x = first_own_ref[:, cols].astype(F32)
        out_ref[:, cols] = (x + dot(hidden, up_own_ref[:, cols])).astype(BF16)


def forward_into(s_ref, x_ref, hidden, up, out_ref, rows):
    count, _, width = up.shape
    size = chunk_of(width)
    for k in range(count):
        for j in range(width // size):
            cols = pl.ds(pl.multiple_of(s_ref[2 + k] * width + j * size, size), size)
            x = x_ref[:, cols].astype(F32)
            out_ref[rows, cols] = (x + dot(hidden, up[k, :, pl.ds(j * size, size)])).astype(BF16)


def factor_from(s_ref, grad_ref, rows, inner, up):
    count, _, width = up.shape
    back_h = dot_nt(grad_ref[rows, columns(s_ref[2], width)], up[0])
    for k in range(1, count):
        back_h += dot_nt(grad_ref[rows, columns(s_ref[2 + k], width)], up[k])
    return factor_of(inner, back_h)


def back_kernel(count, given, s_ref, x_hbm, came_hbm, inner_ref, scale_ref, gain_ref, *refs):
    refs = list(refs)
    factor_in = refs.pop(0) if given else None
    ups, downs, refs = refs[:count], refs[count:2 * count], refs[2 * count:]
    out_hbm = refs.pop(0)
    factor_out = None if given else refs.pop(0)
    x_ref, grad_ref, out_ref, up, down, sems = refs
    rows, full = x_ref.shape
    width = up.shape[2]
    size = chunk_of(width)
    every = pl.ds(0, rows)
    is_last = s_ref[0] == 1
    grad_copy = started(came_hbm, grad_ref, sems.at[0])

    def load_ups():
        return [started(ups[k], up.at[k], sems.at[2 + k]) for k in range(count)]

    up_copies = [] if given else load_ups()
    x_copy = started(x_hbm, x_ref, sems.at[1])
    down_copies = [started(downs[k], down.at[k], sems.at[2 + count + k]) for k in range(count)]
    inner = inner_ref[...]
    grad_copy.wait()
    for copy in up_copies:
        copy.wait()
    if given:
        x_copy.wait()

    @pl.when(is_last)
    def _():
        if given:
            for copy in load_ups():
                copy.wait()
        else:
            x_copy.wait()
        forward_into(s_ref, x_ref, hidden_of(inner), up, grad_ref, every)

    if given:
        factor = factor_in[...]
    else:
        factor = factor_from(s_ref, grad_ref, every, inner, up)
        factor_out[...] = factor

        @pl.when(jnp.logical_not(is_last))
        def _():
            x_copy.wait()

    mean = jnp.sum(factor.astype(F32) * inner, -1, keepdims=True) / full
    scale = scale_ref[:, 0:1]
    bend = scale * scale * mean
    out_copies = []
    for k in range(count):
        down_copies[k].wait()
        for j in range(width // size):
            cols = pl.ds(pl.multiple_of(s_ref[2 + k] * width + j * size, size), size)
            back_n = dot_nt(factor, down[k, pl.ds(j * size, size), :]) * gain_ref[:, cols]
            x = x_ref[:, cols].astype(F32)
            grad = grad_ref[:, cols].astype(F32)
            out_ref[:, cols] = (grad + (scale * back_n - bend * x)).astype(BF16)
        cols = columns(s_ref[2 + k], width)
        out_copies.append(
            started(out_ref.at[:, cols], out_hbm.at[:, cols], sems.at[2 + 2 * count + k])
        )
    for copy in out_copies:
        copy.wait()


def rest_kernel(count, s_ref, first_ref, inner_ref, *refs):
    ups, out_refs = refs[:count], refs[count:]
    width = ups[0].shape[1]
    size = chunk_of(width)
    hidden = hidden_of(inner_ref[...])
    places = [(ref, at) for ref in out_refs for at in range(ref.shape[1] // width)]
    for k, (out_ref, at) in enumerate(places):
        for j in range(width // size):
            cols = pl.ds(pl.multiple_of(s_ref[3 + k] * width + j * size, size), size)
            x = first_ref[:, cols].astype(F32)
            out_ref[:, pl.ds(at * width + j * size, size)] = (
                x + dot(hidden, ups[k][:, pl.ds(j * size, size)])
            ).astype(BF16)


def terms_kernel(
    count, s_ref, stash_hbm, first_hbm, came0_hbm, came1_hbm, inner_s_ref, inner_a_ref,
    factor0_ref, scale_s_ref, scale_a_ref, gain_ref, *refs
):
    ups, refs = refs[:count], refs[count:]
    factor_ref, up_slices, down_slices = refs[0], refs[1:1 + count], refs[1 + count:1 + 2 * count]
    grads, x_s, x_a, up, sems = refs[1 + 2 * count:]
    rows, _ = x_s.shape
    width = up.shape[2]
    size = chunk_of(width)
    first_rows, second_rows = pl.ds(0, rows), pl.ds(rows, rows)
    copies = [started(came1_hbm, grads.at[second_rows], sems.at[0])]
    copies += [started(ups[k], up.at[k], sems.at[4 + k]) for k in range(count)]
    copies += [started(came0_hbm, grads.at[first_rows], sems.at[1])]
    late = [started(stash_hbm, x_s, sems.at[2]), started(first_hbm, x_a, sems.at[3])]
    hidden_s, hidden_a = hidden_of(inner_s_ref[...]), hidden_of(inner_a_ref[...])
    for copy in copies:
        copy.wait()

    @pl.when(s_ref[0] == 1)
    def _():
        for copy in late:
            copy.wait()
        forward_into(s_ref, x_s, hidden_s, up, grads, first_rows)
        forward_into(s_ref, x_a, hidden_a, up, grads, second_rows)

    factor1 = factor_from(s_ref, grads, second_rows, inner_a_ref[...], up)
    factor_ref[...] = factor1
    hidden = jnp.concatenate([hidden_s, hidden_a], 0).astype(F32).T.astype(BF16)
    for k, ref in enumerate(up_slices):
        base = s_ref[2 + count + k] * width
        for j in range(width // size):
            cols = pl.ds(pl.multiple_of(base + j * size, size), size)
            ref[:, pl.ds(j * size, size)] = dot(hidden, grads[:, cols]).astype(ref.dtype)
    factor = jnp.concatenate([factor0_ref[...], factor1], 0)

    @pl.when(s_ref[0] == 0)
    def _():
        for copy in late:
            copy.wait()

    pairs = ((x_s, scale_s_ref[:, 0:1]), (x_a, scale_a_ref[:, 0:1]))
    for k, ref in enumerate(down_slices):
        base = s_ref[2 + count + k] * width
        for j in range(width // size):
            cols = pl.ds(pl.multiple_of(base + j * size, size), size)
            normed = jnp.concatenate(
                [(x[:, cols].astype(F32) * scale * gain_ref[:, cols]).astype(BF16) for x, scale in pairs], 0
            )
            ref[pl.ds(j * size, size), :] = dot_tn(normed, factor).astype(ref.dtype)


def compose_into(x_ref, order, blocks, texts, maps, part_ref, sems):
    rows, _ = x_ref.shape
    size = part_ref.shape[3]
    copies = []
    for half, refs in enumerate((texts, maps)):
        slabs = [(ref, k) for ref in refs for k in range(ref.shape[0])]
        for at, (ref, k) in enumerate(slabs):
            copies.append(started(ref.at[k], part_ref.at[half, at], sems.at[half, at]))
    flat = [ref[k].astype(F32) for ref in blocks for k in range(ref.shape[0])]
    slots = flat[0].shape[0] // 2
    row = lax.broadcasted_iota(jnp.int32, (rows, slots), 0).astype(F32)
    slot = lax.broadcasted_iota(jnp.int32, (rows, slots), 1).astype(F32)
    vision = jnp.zeros((rows, flat[0].shape[1]), F32)
    marked = jnp.zeros((rows, 1), F32)
    for block in flat:
        number, first_row = block[slots:slots + 1, 0:1], block[slots:slots + 1, 1:2]
        placed = jnp.where((row == first_row + slot) & (slot < number), 1.0, 0.0)
        vision += dot(placed.astype(BF16), block[:slots].astype(BF16))
        marked += jnp.sum(placed, -1, keepdims=True)
    vision = vision.astype(BF16)
    for at, section in enumerate(order):
        copies[at].wait()
        copies[len(order) + at].wait()
        mapped = dot(vision, part_ref[1, at])
        text = part_ref[0, at].astype(F32)
        x_ref[:, pl.ds(section * size, size)] = jnp.where(marked > 0.5, mapped, text).astype(BF16)


def last_kernel(count, order, n_arrays, s_ref, gain_ref, own_hbm, *refs):
    refs = list(refs)
    rests, refs = refs[:2], refs[2:]
    blocks, texts, maps = (refs[at * n_arrays:(at + 1) * n_arrays] for at in range(3))
    refs = refs[3 * n_arrays:]
    downs, ups = refs[:count], refs[count:2 * count]
    out_hbm, x_ref, out_ref, up, down, part_ref, sems, part_sems = refs[2 * count:]
    width = up.shape[2]
    rows, full = x_ref.shape
    size = chunk_of(width)

    @pl.when(s_ref[1] == 1)
    def _():
        compose_into(x_ref, order, blocks, texts, maps, part_ref, part_sems)

    @pl.when(s_ref[1] == 0)
    def _():
        copies = [started(own_hbm, x_ref.at[:, columns(s_ref[2], width)], sems.at[0])]
        for ref in rests:
            for at in range(ref.shape[1] // width):
                k = len(copies)
                copies.append(
                    started(
                        ref.at[:, pl.ds(at * width, width)],
                        x_ref.at[:, columns(s_ref[2 + k], width)],
                        sems.at[k],
                    )
                )
        for copy in copies:
            copy.wait()

    down_copies = [started(downs[k], down.at[k], sems.at[count + k]) for k in range(count)]
    up_copies = [started(ups[k], up.at[k], sems.at[2 * count + k]) for k in range(count)]
    scale = scale_into(x_ref, full)
    inner = jnp.zeros((rows, down.shape[2]), F32)
    for k in range(count):
        down_copies[k].wait()
        for j in range(width // size):
            cols = pl.ds(pl.multiple_of(s_ref[2 + k] * width + j * size, size), size)
            normed = (x_ref[:, cols].astype(F32) * scale * gain_ref[:, cols]).astype(BF16)
            inner += dot(normed, down[k, pl.ds(j * size, size), :])
    hidden = hidden_of(inner)
    out_copies = []
    for k in range(count):
        up_copies[k].wait()
        for j in range(width // size):
            cols = pl.ds(pl.multiple_of(s_ref[2 + k] * width + j * size, size), size)
            x = x_ref[:, cols].astype(F32)
            out_ref[:, cols] = (x + dot(hidden, up[k, :, pl.ds(j * size, size)])).astype(BF16)
        cols = columns(s_ref[2 + k], width)
        out_copies.append(
            started(out_ref.at[:, cols], out_hbm.at[:, cols], sems.at[3 * count + k])
        )
    for copy in out_copies:
        copy.wait()


def encode_section(query, keys, values):
    q3 = query.reshape(query.shape[0], HEADS, HEAD_DIM)
    k3 = keys.reshape(keys.shape[0], HEADS, HEAD_DIM)
    v3 = values.reshape(values.shape[0], HEADS, HEAD_DIM)
    scores = jnp.einsum("qhd,khd->hqk", q3, k3, preferred_element_type=F32) * HEAD_DIM ** (-0.5)
    top = jnp.max(scores, -1, keepdims=True)
    weights = jnp.exp(scores - top)
    probs = (weights / jnp.sum(weights, -1, keepdims=True)).astype(BF16)
    attended = jnp.einsum("hqk,khd->qhd", probs, v3, preferred_element_type=F32)
    return attended.reshape(query.shape[0], HEADS * HEAD_DIM).astype(BF16)


def tree_round(held, step):
    length = lax.axis_size("pipe")
    pairs = [(i + at + step, i + at) for i in range(0, length, 2 * step) for at in (0, 1)]
    packed = jnp.stack(held)
    return packed, lax.ppermute(packed, "pipe", pairs)


def tree_start(arrays, step=2):
    length = lax.axis_size("pipe")
    arrays = list(arrays)
    while step < length:
        packed, came = tree_round([a[k] for a in arrays for k in range(a.shape[0])], step)
        if 2 * step == length:
            early = to_first(packed)
        arrays.append(came)
        step *= 2
    order = [0]
    for at in range(1, length.bit_length() - 1):
        order = order + [section + 2**at for section in order]
    return arrays, early, came, order + [section + 1 for section in order]


def to_first(array):
    return lax.ppermute(array, "pipe", [(1, 0)])


def tokens_of(attended, merge_gain, merge_pieces, tok_count, tok_offset):
    slots = attended.shape[0]
    x32 = attended.astype(F32)
    scale = lax.rsqrt(jnp.mean(x32 * x32, -1, keepdims=True) + EPS)
    normed = (x32 * scale * merge_gain).astype(BF16)
    merged = [jax.nn.gelu(dot_nt(normed, piece)).astype(BF16) for piece in merge_pieces]
    size = merged[0].shape[1]
    tokens = jnp.zeros((slots, size * len(merged)), BF16)
    for piece, owner in zip(merged, owners()):
        tokens = lax.dynamic_update_slice_in_dim(tokens, piece, owner * size, 1)
    place = jnp.concatenate([tok_count, tok_offset], 1).astype(BF16)
    place = jnp.pad(place, ((0, slots - 1), (0, tokens.shape[1] - 2)))
    return jnp.concatenate([tokens, place], 0)


def body(
    act_in,
    stash_a,
    grad_in,
    text_emb,
    enc_query,
    enc_key,
    enc_value,
    tok_count,
    tok_offset,
    merge_gain,
    w_merge,
    w_vision,
    norm_gain,
    w_down,
    w_up,
):
    section = lax.axis_index("pipe")
    is_last = section == lax.axis_size("pipe") - 1
    count = lax.axis_size("dp")
    chips = count // 2
    gain = norm_gain
    first, stash, grad = act_in[0, 0], stash_a[0, 0], grad_in[0, 0]
    down, up = w_down[0], w_up[0]
    rows, full = first.shape
    rank, width = up.shape
    n_pipe = lax.axis_size("pipe")
    sent_to, kept_by = targets()
    scalars = jnp.stack(
        [is_last.astype(jnp.int32), (section == 0).astype(jnp.int32)]
        + owners() + sent_to + kept_by
    ).astype(jnp.int32)

    def vmem(dims):
        return pltpu.VMEM(dims, BF16)

    act, ups_shape, downs_shape = (rows, full), (count, rank, width), (count, width, rank)

    down_far = far_pieces(down)
    text_arrays, text_early, text_waiting, order = tree_start([text_emb])
    _, map_came = tree_round([w_vision], 2)
    down_near, up_near = swap_cores(down), swap_cores(up)
    prep_outs = [shape(act, BF16), shape((rows, 128), F32)]
    normed_a, scale_a = call(prep_kernel, scalars, [first, gain], prep_outs)
    normed_s, scale_s = call(prep_kernel, scalars, [stash, gain], prep_outs)
    up = tied(up, normed_a, normed_s, *down_far)
    up_far = far_pieces(up)
    downs = with_far(down, down_near, down_far)

    inner_a, out_own = call(
        functools.partial(forward_kernel, count), scalars, [normed_a, first, up] + downs,
        [shape((rows, rank), F32), shape((rows, width), BF16)],
        in_specs={1: pl.BlockSpec((rows, width), lambda i, s: (0, s[2]))},
    )
    came_own = passed_along(out_own, 1)
    text_arrays += [text_early, to_first(tied(text_waiting, out_own))]
    (inner_s,) = call(
        functools.partial(inner_kernel, count), scalars, [tied(normed_s, out_own)] + downs,
        [shape((rows, rank), F32)],
    )
    query = tied(enc_query[0], out_own)
    attended = encode_section(query, enc_key[0], enc_value[0])

    ups = with_far(up, up_near, up_far)
    back_scratch = [vmem(act)] * 3 + [
        vmem(ups_shape), vmem(downs_shape), pltpu.SemaphoreType.DMA((2 + 3 * count,))
    ]
    hands = set(range(5, 5 + 2 * count)) | {0, 1}
    back0, factor0 = call(
        functools.partial(back_kernel, count, False), scalars,
        [tied(stash, came_own, attended, map_came, *text_arrays[1:]), grad, inner_s, scale_s, gain] + ups + downs,
        [shape(act, BF16), shape((rows, rank), BF16)],
        scratch=back_scratch, by_hand=hands, outs_by_hand={0},
    )
    after = passed_along(back0, -1)

    groups = [1, count - 2]
    rests = call(
        functools.partial(rest_kernel, count - 1), scalars,
        [tied(first, factor0), inner_a] + ups[1:], [shape((rows, group * width), BF16) for group in groups],
    )
    merge_own = tied(w_merge, factor0).T
    merge_pieces = direct_pieces(merge_own)

    tokens = tokens_of(attended, merge_gain, merge_pieces, tok_count, tok_offset)

    after = tied(after, tokens, *rests)
    came_rests, before = [], after
    for rest in rests:
        before = passed_along(tied(rest, before), 1)
        came_rests.append(before)
    map_came = tied(map_came, after)
    if n_pipe == 8:
        packed = jnp.stack([w_vision, map_came[0]])
        from_one = to_first(packed)
        from_four = lax.ppermute(packed, "pipe", [(4, 0)])
        from_five = lax.ppermute(tied(packed, from_one), "pipe", [(5, 0)])
        map_arrays = [w_vision[None], map_came, from_four, from_one, from_five]
    else:
        map_arrays, map_early, map_waiting, _ = tree_start([w_vision[None], map_came], 4)
        map_arrays += [map_early, to_first(map_waiting)]

    ups_out = [shape((rank, width), BF16)] * chips + [shape((rank, width), F32)] * chips
    downs_out = [shape((width, rank), BF16)] * chips + [shape((width, rank), F32)] * chips
    factor1, *slices = call(
        functools.partial(terms_kernel, count), scalars,
        [stash, first, grad, after, inner_s, inner_a, factor0, scale_s, scale_a, gain] + ups,
        [shape((rows, rank), BF16)] + ups_out + downs_out,
        scratch=[
            vmem((2 * rows, full)), vmem(act), vmem(act), vmem(ups_shape),
            pltpu.SemaphoreType.DMA((4 + count,)),
        ],
        by_hand={0, 1, 2, 3} | set(range(10, 10 + count)), room=58,
    )
    up_slices, down_slices = slices[:count], slices[count:]
    sums = []
    for slices in (up_slices, down_slices):
        sent, kept = slices[:chips], slices[chips:]
        terms = [kept[0] + swap_cores(sent[0]).astype(F32)]
        for k in range(chips - 1, 0, -1):
            far = (kept[k] + swap_cores(sent[k]).astype(F32)).astype(BF16)
            terms.append(shift_chips(far, k))
        sums.append(terms)
    token_arrays, token_early, token_waiting, _ = tree_start([tied(tokens, after)[None]])
    (back1,) = call(
        functools.partial(back_kernel, count, True), scalars,
        [first, after, inner_a, scale_a, gain, factor1] + ups + downs,
        [shape(act, BF16)],
        scratch=back_scratch, by_hand=set(range(6, 6 + 2 * count)) | {0, 1}, outs_by_hand={0},
    )

    token_arrays += [token_early, to_first(token_waiting)]
    n_arrays = len(token_arrays)
    blocks_at = 2 + len(came_rests)
    (out1,) = call(
        functools.partial(last_kernel, count, order, n_arrays), scalars,
        [gain, came_own] + came_rests + token_arrays + text_arrays + map_arrays + downs + ups, [shape(act, BF16)],
        scratch=[vmem(act)] * 2 + [
            vmem(ups_shape), vmem(downs_shape), vmem((2, n_pipe) + w_vision.shape),
            pltpu.SemaphoreType.DMA((4 * count,)), pltpu.SemaphoreType.DMA((2, n_pipe)),
        ],
        by_hand=set(range(1, blocks_at)) | set(range(blocks_at + n_arrays, blocks_at + 3 * n_arrays + 2 * count)), outs_by_hand={0},
        room=18,
    )
    grad_up, grad_down = (
        sum((tied(term, out1).astype(F32) for term in terms[1:]), terms[0]) for terms in sums
    )
    return (out1[None, None], back1[None, None], grad_down[None], grad_up[None])


def solution(mesh):
    in_specs = (
        P("dp", "pipe", None, None),
        P("dp", "pipe", None, None),
        P("dp", "pipe", None, None),
        P("dp", None, "pipe"),
        P("dp", "pipe", None),
        P("dp", "pipe", None),
        P("dp", "pipe", None),
        P("dp", "pipe"),
        P("dp", "pipe"),
        P(),
        P(None, "dp"),
        P(None, "pipe"),
        P("pipe", None),
        P("pipe", "dp", None),
        P("pipe", None, "dp"),
    )
    out_specs = (
        P("dp", "pipe", None, None),
        P("dp", "pipe", None, None),
        P("pipe", "dp", None),
        P("pipe", None, "dp"),
    )
    return jax.shard_map(body, mesh=mesh, in_specs=in_specs, out_specs=out_specs, check_vma=False)
```
